32 devices in a mesh: head: 1, seq: 32 (over z, y, x, core).
Axes of the slice: x: 2, y: 2, z: 4, core: 2. Of those that a mesh axis runs over, the one named last changes fastest.
Arguments:
- queries: bfloat16 [8192, 4096], P('seq', 'head'), may hold values from -6 to 6
- keys: bfloat16 [8192, 4096], P('seq', 'head'), may hold values from -6 to 6
- values: bfloat16 [8192, 4096], P('seq', 'head'), may hold values from -6 to 6
- token_rates: float32 [16, 8192], P('head', 'seq'), may hold values from 0.05 to 1
- w_gate: bfloat16 [16, 256, 512], P('head'), may hold values from -6 to 6
- w_up: bfloat16 [16, 256, 512], P('head'), may hold values from -6 to 6
- w_down: bfloat16 [16, 512, 256], P('head'), may hold values from -6 to 6
Outputs:
- applied: bfloat16 [8192, 4096], P('seq', 'head')
- step_gate: bfloat16 [16, 256, 512], P('head')
- step_up: bfloat16 [16, 256, 512], P('head')
- step_down: bfloat16 [16, 256, 512], P('head')
The draws below stay inside these ranges and needn't reach their ends.
All inputs are finite; a program needn't handle non-finite values.
Results may differ from the reference program's by a relative error of at most 0.035.
Values may be sent and summed in bfloat16 or wider, within the bound.
No kernel may reach another device: no remote copies, remote signals or barrier semaphores. Data moves between devices by JAX's collectives and lax.ppermute only.
A program may use at most 192 MiB of HBM per device.

```python
import math
import jax
import jax.numpy as jnp

HEADS = 16
DH = 256
HID = 512
NS_STEPS = 5
SEQ_LEN = 8192


def steps_of(own_key, dims, split, least, largest):
    loudness, own = 1.0, jax.random.fold_in(own_key, 6)
    for axis_at, shards_of in split:
        heights = jnp.exp(jax.random.uniform(jax.random.fold_in(own, axis_at), (shards_of,), jnp.float32, least / len(split), largest / len(split)))
        loudness = loudness * jnp.repeat(heights, dims[axis_at] // shards_of).reshape([-1 if axis == axis_at else 1 for axis in range(len(dims))])
    return loudness


def centred(rng, dims, width, bound, shards=(), held_as=jnp.bfloat16):
    factor_of = steps_of(rng, dims, shards, -0.22, 0.18) if shards else 1.0
    values = jax.random.normal(rng, dims, jnp.float32) * width * factor_of
    return jnp.minimum(jnp.maximum(values, -bound), bound).astype(held_as)


def setup_inputs(seed: int = 0) -> dict:
    splits = jax.random.split(jax.random.key(seed), 8)
    return {
        "queries": centred(splits[0], (SEQ_LEN, HEADS * DH), 1.0, 6.0, ((0, 32),)),
        "keys": centred(splits[1], (SEQ_LEN, HEADS * DH), 1.0, 6.0, ((0, 32),)),
        "values": centred(splits[2], (SEQ_LEN, HEADS * DH), 1.0, 6.0, ((0, 32),)),
        "token_rates": jnp.clip(jnp.exp(math.log(1.0) - 2.9957323 * jax.random.uniform(splits[3], (HEADS, SEQ_LEN), jnp.float32) ** steps_of(splits[3], (HEADS, SEQ_LEN), ((1, 32),), -0.2, 0.2)), 0.05, 1.0),
        "w_gate": centred(splits[4], (HEADS, DH, HID), 1.0, 6.0),
        "w_up": centred(splits[5], (HEADS, DH, HID), 1.0, 6.0),
        "w_down": centred(splits[6], (HEADS, HID, DH), 1.0, 6.0),
    }


def newton(grad):
    norm = jnp.sqrt(jnp.sum(grad * grad))
    xmat = (grad / (norm + 1e-07)).astype(jnp.bfloat16)
    for step in range(NS_STEPS):
        amat = jnp.dot(xmat, xmat.T, preferred_element_type=jnp.float32).astype(jnp.bfloat16)
        bmat = (-4.775 * amat.astype(jnp.float32) + 2.0315 * jnp.dot(amat, amat, preferred_element_type=jnp.float32)).astype(jnp.bfloat16)
        nxt = 3.4445 * xmat.astype(jnp.float32) + jnp.dot(bmat, xmat, preferred_element_type=jnp.float32)
        if step == NS_STEPS - 1:
            nxt = nxt * (0.2 * math.sqrt(HID))
        xmat = nxt.astype(jnp.bfloat16)
    return xmat

def reference(queries, keys, values, token_rates, w_gate, w_up, w_down):
    scale_one = DH ** (-0.5)
    scale_two = HID ** (-0.5)
    outs_list, gate_list, up_list, down_list = ([], [], [], [])
    for head in range(HEADS):
        cols = slice(head * DH, (head + 1) * DH)
        qpart, kpart, vpart = (queries[:, cols], keys[:, cols], values[:, cols])
        gq = scale_one * jnp.dot(qpart, w_gate[head], preferred_element_type=jnp.float32)
        uq = scale_one * jnp.dot(qpart, w_up[head], preferred_element_type=jnp.float32)
        hq = (jax.nn.silu(gq) * uq).astype(jnp.bfloat16)
        outs_list.append((scale_two * jnp.dot(hq, w_down[head], preferred_element_type=jnp.float32)).astype(jnp.bfloat16))
        gk = scale_one * jnp.dot(kpart, w_gate[head], preferred_element_type=jnp.float32)
        uk = scale_one * jnp.dot(kpart, w_up[head], preferred_element_type=jnp.float32)
        hk = (jax.nn.silu(gk) * uk).astype(jnp.bfloat16)
        vrate = (token_rates[head][:, None] * vpart.astype(jnp.float32)).astype(jnp.bfloat16)
        gdown = -scale_two * jnp.dot(vrate.T, hk, preferred_element_type=jnp.float32)
        dhid = -scale_two * jnp.dot(vrate, w_down[head].T, preferred_element_type=jnp.float32)
        sig = jax.nn.sigmoid(gk)
        dgate = (dhid * uk * sig * (1.0 + gk * (1.0 - sig))).astype(jnp.bfloat16)
        dup = (dhid * jax.nn.silu(gk)).astype(jnp.bfloat16)
        ggate = scale_one * jnp.dot(kpart.T, dgate, preferred_element_type=jnp.float32)
        gup = scale_one * jnp.dot(kpart.T, dup, preferred_element_type=jnp.float32)
        gate_list.append(newton(ggate))
        up_list.append(newton(gup))
        down_list.append(newton(gdown))
    return (jnp.concatenate(outs_list, axis=1), jnp.stack(gate_list), jnp.stack(up_list), jnp.stack(down_list))
```

```python
import functools
import math

import jax
import jax.numpy as jnp
from jax import lax
from jax.experimental import pallas as pl
from jax.experimental.pallas import tpu as pltpu
from jax.sharding import PartitionSpec as P

NS_STEPS = 5
BF = jnp.bfloat16
F32 = jnp.float32
VMEM_BYTES = 48 * 1024 * 1024
ANY = pl.BlockSpec(memory_space=pl.ANY)
SMEM = pl.BlockSpec(memory_space=pltpu.SMEM)

NZ = 4
PLANE = 8
DEVICES = NZ * PLANE


def newton_batch(xmat, width):
    for step in range(NS_STEPS):
        amat = jnp.einsum("mdf,mef->mde", xmat, xmat, preferred_element_type=F32).astype(BF)
        square = jnp.einsum("mde,mef->mdf", amat, amat, preferred_element_type=F32)
        bmat = (-4.775 * amat.astype(F32) + 2.0315 * square).astype(BF)
        nxt = 3.4445 * xmat.astype(F32) + jnp.einsum(
            "mde,mef->mdf", bmat, xmat, preferred_element_type=F32
        )
        if step == NS_STEPS - 1:
            nxt = nxt * (0.2 * math.sqrt(width))
        xmat = nxt.astype(BF)
    return xmat


def per_device_plain(queries, keys, values, token_rates, w_gate, w_up, w_down):
    head_count, head_size, hidden = w_gate.shape
    tokens = queries.shape[0]
    scale_one = head_size ** (-0.5)
    scale_two = hidden ** (-0.5)
    qpart = queries.reshape(tokens, head_count, head_size)
    kpart = keys.reshape(tokens, head_count, head_size)
    vpart = values.reshape(tokens, head_count, head_size)
    gq = scale_one * jnp.einsum("thd,hdf->htf", qpart, w_gate, preferred_element_type=F32)
    uq = scale_one * jnp.einsum("thd,hdf->htf", qpart, w_up, preferred_element_type=F32)
    hq = (jax.nn.silu(gq) * uq).astype(BF)
    applied = (
        scale_two * jnp.einsum("htf,hfd->thd", hq, w_down, preferred_element_type=F32)
    ).astype(BF)
    applied = applied.reshape(tokens, head_count * head_size)
    gk = scale_one * jnp.einsum("thd,hdf->htf", kpart, w_gate, preferred_element_type=F32)
    uk = scale_one * jnp.einsum("thd,hdf->htf", kpart, w_up, preferred_element_type=F32)
    hk = (jax.nn.silu(gk) * uk).astype(BF)
    vrate = (jnp.transpose(token_rates)[:, :, None] * vpart.astype(F32)).astype(BF)
    gdown = -scale_two * jnp.einsum("thd,htf->hdf", vrate, hk, preferred_element_type=F32)
    dhid = -scale_two * jnp.einsum("thd,hfd->htf", vrate, w_down, preferred_element_type=F32)
    sig = jax.nn.sigmoid(gk)
    dgate = (dhid * uk * sig * (1.0 + gk * (1.0 - sig))).astype(BF)
    dup = (dhid * jax.nn.silu(gk)).astype(BF)
    ggate = scale_one * jnp.einsum("thd,htf->hdf", kpart, dgate, preferred_element_type=F32)
    gup = scale_one * jnp.einsum("thd,htf->hdf", kpart, dup, preferred_element_type=F32)
    total = lax.psum(jnp.stack([ggate, gup, gdown], axis=1), "seq")
    norms = jnp.sqrt(jnp.sum(total * total, axis=(2, 3)))
    xmat = (total / (norms[:, :, None, None] + 1e-07)).astype(BF)
    result = newton_batch(xmat.reshape(head_count * 3, head_size, hidden), hidden)
    result = result.reshape(head_count, 3, head_size, hidden)
    return (applied, result[:, 0], result[:, 1], result[:, 2])


def sigmoid(x):
    return 0.5 * jnp.tanh(0.5 * x) + 0.5


def dot(a, b, dims=((1,), (0,))):
    return lax.dot_general(a, b, (dims, ((), ())), preferred_element_type=F32)


def applied_kernel(scale_one, scale_two, q_ref, wg_ref, wu_ref, wd_ref, out_ref):
    q = q_ref[...]
    gq = scale_one * dot(q, wg_ref[0])
    hq = (gq * sigmoid(gq) * (scale_one * dot(q, wu_ref[0]))).astype(BF)
    out_ref[...] = (scale_two * dot(hq, wd_ref[0])).astype(BF)


def apply_queries(queries, w_gate, w_up, w_down):
    heads, size, hidden = w_gate.shape
    tokens = queries.shape[0]
    return pl.pallas_call(
        functools.partial(applied_kernel, size**-0.5, hidden**-0.5),
        grid=(heads,),
        out_shape=jax.ShapeDtypeStruct(queries.shape, BF),
        in_specs=[
            pl.BlockSpec((tokens, size), lambda h: (0, h)),
            pl.BlockSpec((1, size, hidden), lambda h: (h, 0, 0)),
            pl.BlockSpec((1, size, hidden), lambda h: (h, 0, 0)),
            pl.BlockSpec((1, hidden, size), lambda h: (h, 0, 0)),
        ],
        out_specs=pl.BlockSpec((tokens, size), lambda h: (0, h)),
        compiler_params=pltpu.CompilerParams(vmem_limit_bytes=VMEM_BYTES),
        cost_estimate=pl.CostEstimate(
            flops=6 * heads * tokens * size * hidden,
            bytes_accessed=4 * queries.size + 6 * w_gate.size,
            transcendentals=heads * tokens * hidden,
        ),
        name="apply_queries",
    )(queries, w_gate, w_up, w_down)


def pack_kernel(size, where_ref, k_ref, v_ref, rate_ref, *rest):
    outs, packed, sem = rest[:PLANE], rest[PLANE], rest[PLANE + 1]
    rates = jnp.transpose(rate_ref[...])
    for head in range(PLANE):
        cols = slice(head * size, (head + 1) * size)
        packed[head, 0] = k_ref[:, cols]
        packed[head, 1] = (rates[:, head : head + 1] * v_ref[:, cols].astype(F32)).astype(BF)
    mine = where_ref[0]
    copies = [
        pltpu.make_async_copy(packed.at[mine ^ d], outs[d], sem.at[d]) for d in range(PLANE)
    ]
    for copy in copies:
        copy.start()
    for copy in copies:
        copy.wait()


def pack_tokens(where, keys, values, rates, group, size):
    tokens = keys.shape[0]
    cols = PLANE * size
    return pl.pallas_call(
        functools.partial(pack_kernel, size),
        grid=(1,),
        out_shape=[jax.ShapeDtypeStruct((2, tokens, size), BF)] * PLANE,
        in_specs=[
            SMEM,
            pl.BlockSpec((tokens, cols), lambda i: (0, group)),
            pl.BlockSpec((tokens, cols), lambda i: (0, group)),
            pl.BlockSpec((PLANE, tokens), lambda i: (group, 0)),
        ],
        out_specs=[ANY] * PLANE,
        scratch_shapes=[
            pltpu.VMEM((PLANE, 2, tokens, size), BF),
            pltpu.SemaphoreType.DMA((PLANE,)),
        ],
        compiler_params=pltpu.CompilerParams(vmem_limit_bytes=VMEM_BYTES),
        cost_estimate=pl.CostEstimate(
            flops=tokens * cols, bytes_accessed=8 * tokens * cols, transcendentals=0
        ),
        name="pack_tokens",
    )(where, keys, values, rates)


def grads_kernel(scale_one, scale_two, where_ref, wg_ref, wu_ref, wd_ref, *rest):
    blocks, rest = rest[:PLANE], rest[PLANE:]
    outs, (held, total, final, sem) = rest[:NZ], rest[NZ:]
    copies = [
        pltpu.make_async_copy(blocks[b], held.at[b], sem.at[b]) for b in range(PLANE)
    ]
    for copy in copies:
        copy.start()
    wg, wu = wg_ref[0], wu_ref[0]
    wdt = jnp.transpose(wd_ref[0])
    for copy in copies:
        copy.wait()

    def step(b, carry):
        k, vr = held[b, 0], held[b, 1]
        gk = scale_one * dot(k, wg)
        uk = dot(k, wu)
        dh = dot(vr, wdt)
        sig = sigmoid(gk)
        act = gk * sig
        hk = (act * uk).astype(BF)
        dg = (dh * uk * (sig + act * (1.0 - sig))).astype(BF)
        du = (dh * act).astype(BF)
        kt, vt = jnp.transpose(k), jnp.transpose(vr)
        parts = (dot(kt, dg), dot(kt, du), dot(vt, hk))

        @pl.when(b == 0)
        def _():
            for i in range(3):
                total[i] = parts[i]

        @pl.when(b > 0)
        def _():
            for i in range(3):
                total[i] += parts[i]

        return carry

    lax.fori_loop(0, PLANE, step, 0)
    both = -scale_one * scale_two
    down = (both * total[2]).astype(BF)
    final[0] = (both * scale_one * total[0]).astype(BF)
    final[1] = down
    final[2] = (both * total[1]).astype(BF)
    final[3] = down
    own_z = where_ref[1]
    copies = [pltpu.make_async_copy(final.at[own_z ^ r], outs[r], sem.at[r]) for r in range(NZ)]
    for copy in copies:
        copy.start()
    for copy in copies:
        copy.wait()


def head_grads(where, blocks, w_gate, w_up, w_down, group):
    _, size, hidden = w_gate.shape
    tokens = blocks[0].shape[1]
    rows = tokens * PLANE
    pick = lambda i, where: (group * PLANE + where[0], 0, 0)
    return pl.pallas_call(
        functools.partial(grads_kernel, size**-0.5, hidden**-0.5),
        out_shape=[jax.ShapeDtypeStruct((size, hidden), BF)] * NZ,
        grid_spec=pltpu.PrefetchScalarGridSpec(
            num_scalar_prefetch=1,
            grid=(1,),
            in_specs=[
                pl.BlockSpec((1, size, hidden), pick),
                pl.BlockSpec((1, size, hidden), pick),
                pl.BlockSpec((1, hidden, size), pick),
            ]
            + [ANY] * PLANE,
            out_specs=[ANY] * NZ,
            scratch_shapes=[
                pltpu.VMEM((PLANE, 2, tokens, size), BF),
                pltpu.VMEM((3, size, hidden), F32),
                pltpu.VMEM((NZ, size, hidden), BF),
                pltpu.SemaphoreType.DMA((PLANE,)),
            ],
        ),
        compiler_params=pltpu.CompilerParams(vmem_limit_bytes=VMEM_BYTES),
        cost_estimate=pl.CostEstimate(
            flops=12 * rows * size * hidden,
            bytes_accessed=4 * rows * size + 14 * size * hidden,
            transcendentals=rows * hidden,
        ),
        name="head_grads",
    )(where, w_gate, w_up, w_down, *blocks)


def newton_kernel(a_ref, b_ref, c_ref, d_ref, out_ref):
    width = out_ref.shape[1]
    grad = (a_ref[...].astype(F32) + b_ref[...].astype(F32)) + (
        c_ref[...].astype(F32) + d_ref[...].astype(F32)
    )
    norm = jnp.sqrt(jnp.sum(grad * grad))
    x = (grad / (norm + 1e-07)).astype(BF)
    for step in range(NS_STEPS):
        a = dot(x, x, ((1,), (1,))).astype(BF)
        b = (-4.775 * a.astype(F32) + 2.0315 * dot(a, a)).astype(BF)
        nxt = 3.4445 * x.astype(F32) + dot(b, x)
        if step == NS_STEPS - 1:
            nxt = nxt * (0.2 * math.sqrt(width))
        x = nxt.astype(BF)
    out_ref[...] = x


def newton(parts):
    size, hidden = parts[0].shape
    return pl.pallas_call(
        newton_kernel,
        out_shape=jax.ShapeDtypeStruct((size, hidden), BF),
        compiler_params=pltpu.CompilerParams(vmem_limit_bytes=VMEM_BYTES),
        cost_estimate=pl.CostEstimate(
            flops=NS_STEPS * (4 * size * size * hidden + 2 * size**3),
            bytes_accessed=10 * size * hidden,
            transcendentals=0,
        ),
        name="newton_schulz",
    )(*parts)


def place_kernel(first, group, slot, size, where_ref, *rest):
    own, sibling = rest[:4], rest[4:8]
    gate, up, down, sem = rest[-4:]
    z, y, x, core = (where_ref[i] for i in range(1, 5))
    source_z = z ^ slot
    cut = 3 * size // 4
    tail = size - cut
    half = size // 2

    def put(m0, blocks_zero, blocks_one):
        zero_at = ((y, x), (y ^ 1, x), (y, x ^ 1), (y ^ 1, x ^ 1))
        one_at = ((y, x), (y, x ^ 1), (y ^ 1, x), (y ^ 1, x ^ 1))
        copies = []
        for at, block in zip(zero_at, blocks_zero):
            head = group * PLANE + at[0] * 4 + at[1] * 2 + source_z // 2
            copies.append((block, m0.at[head, pl.ds(0, cut)]))
        for at, block in zip(one_at, blocks_one):
            head = group * PLANE + at[0] * 4 + at[1] * 2 + source_z // 2
            rows = pl.ds(pl.multiple_of(lax.rem(source_z, 2) * half, half), half)
            copies.append((block.at[pl.ds(0, tail)], m0.at[head, pl.ds(cut, tail)]))
            copies.append((block.at[pl.ds(tail, half)], down.at[head, rows]))
        copies = [pltpu.make_async_copy(a, b, sem.at[i]) for i, (a, b) in enumerate(copies)]
        for copy in copies:
            copy.start()
        for copy in copies:
            copy.wait()

    for parity, m0 in ((0, gate), (1, up)):
        for side in range(2):

            @pl.when((lax.rem(source_z, 2) == parity) & (core == side))
            def _():
                pair = (own, sibling) if side == 0 else (sibling, own)
                put(m0, *pair)


def place(where, own, sibling, steps, shape, group, slot):
    size = shape[1]
    first = steps is None
    arrays = () if first else steps
    return pl.pallas_call(
        functools.partial(place_kernel, first, group, slot, size),
        out_shape=[jax.ShapeDtypeStruct(shape, BF)] * 3,
        in_specs=[SMEM] + [ANY] * (8 + len(arrays)),
        out_specs=[ANY] * 3,
        scratch_shapes=[pltpu.SemaphoreType.DMA((12,))],
        input_output_aliases={} if first else {9 + i: i for i in range(3)},
        compiler_params=pltpu.CompilerParams(vmem_limit_bytes=VMEM_BYTES),
        cost_estimate=pl.CostEstimate(
            flops=0, bytes_accessed=4 * 8 * own[0].size, transcendentals=0
        ),
        name="place_steps",
    )(where, *own, *sibling, *arrays)


def permutation(target):
    pairs = []
    for i in range(DEVICES):
        z, y, x, core = target(i // 8, i // 4 % 2, i // 2 % 2, i % 2)
        pairs.append((i, ((z * 2 + y) * 2 + x) * 2 + core))
    return pairs


PLANE_MOVES = [
    permutation(lambda z, y, x, c, d=d: (z, y ^ (d >> 2), x ^ (d >> 1 & 1), c ^ (d & 1)))
    for d in range(PLANE)
]
REDUCE_MOVES = [
    permutation(lambda z, y, x, c, r=r: (2 * c + ((z ^ r) >> 1), y, x, (z ^ r) & 1))
    for r in range(NZ)
]
Z_MOVES = [permutation(lambda z, y, x, c, s=s: (z ^ s, y, x, c)) for s in range(NZ)]
FIRST_MOVE = permutation(lambda z, y, x, c: (z, y ^ (1 - c), x ^ c, c))
SECOND_MOVE = permutation(lambda z, y, x, c: (z, y ^ c, x ^ (1 - c), c))
CORE_MOVE = PLANE_MOVES[1]


def move(array, pairs):
    return lax.ppermute(array, "seq", pairs)


def after(array, *others):
    return lax.optimization_barrier((array, *others))[0]


def per_device_fast(queries, keys, values, token_rates, w_gate, w_up, w_down):
    heads, size, hidden = w_gate.shape
    groups = heads // PLANE
    index = lax.axis_index("seq")
    z, core = index // 8, index % 2
    where = jnp.stack([index % 8, z, index // 4 % 2, index // 2 % 2, core]).astype(jnp.int32)

    applied = apply_queries(queries, w_gate, w_up, w_down)

    received = []
    for group in range(groups):
        blocks = pack_tokens(where, keys, values, token_rates, group, size)
        if group:
            blocks = lax.optimization_barrier((*blocks, received[-1][1]))[:PLANE]
        received.append([blocks[0]] + [move(blocks[d], PLANE_MOVES[d]) for d in range(1, PLANE)])

    steps = None
    cut = 3 * size // 4
    for group in range(groups):
        parts = head_grads(where, received[group], w_gate, w_up, w_down, group)
        parts = [move(parts[r], REDUCE_MOVES[r]) for r in range(NZ)]
        xmat = newton(parts)
        tail = move(xmat[cut:], CORE_MOVE)
        part = lax.dynamic_slice_in_dim(xmat, z % 2 * (size // 2), size // 2, 0)
        payload = jnp.where(core == 0, xmat[:cut], jnp.concatenate([tail, part], 0))
        slots = [payload]
        for s in range(1, NZ):
            slots.append(move(after(payload, slots[-1]), Z_MOVES[s]))
        for s in range(NZ):
            one = move(slots[s], FIRST_MOVE)
            two = move(slots[s], SECOND_MOVE)
            three = move(one, SECOND_MOVE)
            own = [slots[s], one, two, three]
            sibling = [move(b, CORE_MOVE) for b in own]
            steps = place(where, own, sibling, steps, w_gate.shape, group, s)
    return (applied, *steps)


def solution(mesh):
    in_specs = (
        P("seq", "head"),
        P("seq", "head"),
        P("seq", "head"),
        P("head", "seq"),
        P("head", None, None),
        P("head", None, None),
        P("head", None, None),
    )
    out_specs = (
        P("seq", "head"),
        P("head", None, None),
        P("head", None, None),
        P("head", None, None),
    )
    sizes = mesh.shape

    def per_device(*args):
        heads = args[4].shape[0]
        fast = sizes["seq"] == DEVICES and heads % PLANE == 0
        return (per_device_fast if fast else per_device_plain)(*args)

    return jax.shard_map(
        per_device, mesh=mesh, in_specs=in_specs, out_specs=out_specs, check_vma=False
    )
```

```python
import functools
import math

import jax
import jax.numpy as jnp
from jax import lax
from jax.experimental import pallas as pl
from jax.experimental.pallas import tpu as pltpu
from jax.sharding import PartitionSpec as P

NS_STEPS = 5
BF = jnp.bfloat16
F32 = jnp.float32
VMEM_BYTES = 60 * 1024 * 1024

def cost(us):
    return pl.CostEstimate(flops=1, bytes_accessed=int(us * 3.3e6) + 1, transcendentals=0)


COST_APPLY = cost(0)
COST_PACK = cost(0)
COST_GRADS = cost(0)
COST_ADD = cost(0)
COST_NEWTON = cost(0)
COST_PLACE = cost(0)

HBM = pl.BlockSpec(memory_space=pltpu.HBM)
ANY = pl.BlockSpec(memory_space=pl.ANY)
SMEM = pl.BlockSpec(memory_space=pltpu.SMEM)
VMEM = pl.BlockSpec(memory_space=pltpu.VMEM)

NZ = 4
PLANE = 8
DEVICES = NZ * PLANE
SENDS = 2


def newton_batch(xmat, width):
    for step in range(NS_STEPS):
        amat = jnp.einsum("mdf,mef->mde", xmat, xmat, preferred_element_type=F32).astype(BF)
        square = jnp.einsum("mde,mef->mdf", amat, amat, preferred_element_type=F32)
        bmat = (-4.775 * amat.astype(F32) + 2.0315 * square).astype(BF)
        nxt = 3.4445 * xmat.astype(F32) + jnp.einsum(
            "mde,mef->mdf", bmat, xmat, preferred_element_type=F32
        )
        if step == NS_STEPS - 1:
            nxt = nxt * (0.2 * math.sqrt(width))
        xmat = nxt.astype(BF)
    return xmat


def per_device_plain(queries, keys, values, token_rates, w_gate, w_up, w_down):
    head_count, head_size, hidden = w_gate.shape
    tokens = queries.shape[0]
    scale_one = head_size ** (-0.5)
    scale_two = hidden ** (-0.5)
    qpart = queries.reshape(tokens, head_count, head_size)
    kpart = keys.reshape(tokens, head_count, head_size)
    vpart = values.reshape(tokens, head_count, head_size)
    gq = scale_one * jnp.einsum("thd,hdf->htf", qpart, w_gate, preferred_element_type=F32)
    uq = scale_one * jnp.einsum("thd,hdf->htf", qpart, w_up, preferred_element_type=F32)
    hq = (jax.nn.silu(gq) * uq).astype(BF)
    applied = (
        scale_two * jnp.einsum("htf,hfd->thd", hq, w_down, preferred_element_type=F32)
    ).astype(BF)
    applied = applied.reshape(tokens, head_count * head_size)
    gk = scale_one * jnp.einsum("thd,hdf->htf", kpart, w_gate, preferred_element_type=F32)
    uk = scale_one * jnp.einsum("thd,hdf->htf", kpart, w_up, preferred_element_type=F32)
    hk = (jax.nn.silu(gk) * uk).astype(BF)
    vrate = (jnp.transpose(token_rates)[:, :, None] * vpart.astype(F32)).astype(BF)
    gdown = -scale_two * jnp.einsum("thd,htf->hdf", vrate, hk, preferred_element_type=F32)
    dhid = -scale_two * jnp.einsum("thd,hfd->htf", vrate, w_down, preferred_element_type=F32)
    sig = jax.nn.sigmoid(gk)
    dgate = (dhid * uk * sig * (1.0 + gk * (1.0 - sig))).astype(BF)
    dup = (dhid * jax.nn.silu(gk)).astype(BF)
    ggate = scale_one * jnp.einsum("thd,htf->hdf", kpart, dgate, preferred_element_type=F32)
    gup = scale_one * jnp.einsum("thd,htf->hdf", kpart, dup, preferred_element_type=F32)
    total = lax.psum(jnp.stack([ggate, gup, gdown], axis=1), "seq")
    norms = jnp.sqrt(jnp.sum(total * total, axis=(2, 3)))
    xmat = (total / (norms[:, :, None, None] + 1e-07)).astype(BF)
    result = newton_batch(xmat.reshape(head_count * 3, head_size, hidden), hidden)
    result = result.reshape(head_count, 3, head_size, hidden)
    return (applied, result[:, 0], result[:, 1], result[:, 2])


def sigmoid(x):
    return 0.5 * jnp.tanh(0.5 * x) + 0.5


def dot(a, b, dims=((1,), (0,))):
    return lax.dot_general(a, b, (dims, ((), ())), preferred_element_type=F32)


def applied_kernel(scale_one, scale_two, q_ref, wg_ref, wu_ref, wd_ref, out_ref):
    heads, size, _ = wg_ref.shape
    for head in range(heads):
        cols = slice(head * size, (head + 1) * size)
        q = q_ref[:, cols]
        gq = scale_one * dot(q, wg_ref[head])
        hq = (gq * sigmoid(gq) * dot(q, wu_ref[head])).astype(BF)
        out_ref[:, cols] = (scale_one * scale_two * dot(hq, wd_ref[head])).astype(BF)


def apply_queries(queries, w_gate, w_up, w_down):
    heads, size, hidden = w_gate.shape
    tokens = queries.shape[0]
    each = 4
    return pl.pallas_call(
        functools.partial(applied_kernel, size**-0.5, hidden**-0.5),
        grid=(heads // each,),
        out_shape=jax.ShapeDtypeStruct(queries.shape, BF),
        in_specs=[
            pl.BlockSpec((tokens, each * size), lambda h: (0, h)),
            pl.BlockSpec((each, size, hidden), lambda h: (h, 0, 0)),
            pl.BlockSpec((each, size, hidden), lambda h: (h, 0, 0)),
            pl.BlockSpec((each, hidden, size), lambda h: (h, 0, 0)),
        ],
        out_specs=pl.BlockSpec((tokens, each * size), lambda h: (0, h)),
        compiler_params=pltpu.CompilerParams(vmem_limit_bytes=VMEM_BYTES),
        cost_estimate=COST_APPLY,
        name="apply_queries",
    )(queries, w_gate, w_up, w_down)


def pack_kernel(size, k_ref, v_ref, rate_ref, *rest):
    out_ref = rest[-1]
    rates = jnp.transpose(rate_ref[...])
    for head in range(PLANE):
        cols = slice(head * size, (head + 1) * size)
        out_ref[head, 0] = k_ref[:, cols]
        out_ref[head, 1] = (rates[:, head : head + 1] * v_ref[:, cols].astype(F32)).astype(BF)


def pack_tokens(keys, values, rates, group, size, *follows):
    tokens = keys.shape[0]
    cols = PLANE * size
    return pl.pallas_call(
        functools.partial(pack_kernel, size),
        grid=(1,),
        out_shape=jax.ShapeDtypeStruct((PLANE, 2, tokens, size), BF),
        in_specs=[
            pl.BlockSpec((tokens, cols), lambda i: (0, group)),
            pl.BlockSpec((tokens, cols), lambda i: (0, group)),
            pl.BlockSpec((PLANE, tokens), lambda i: (group, 0)),
        ]
        + [ANY] * len(follows),
        out_specs=pl.BlockSpec((PLANE, 2, tokens, size), lambda i: (0, 0, 0, 0)),
        compiler_params=pltpu.CompilerParams(vmem_limit_bytes=VMEM_BYTES),
        cost_estimate=COST_PACK,
        name="pack_tokens",
    )(keys, values, rates, *follows)


def grads_kernel(group, scale_one, scale_two, where_ref, wg_ref, wu_ref, wd_ref, blocks, *rest):
    keep, *send = rest[-9 - SENDS : -8]
    held, total, final, wg_held, wu_held, wd_held, in_sem, sem = rest[-8:]
    head = group * PLANE + where_ref[0]
    weights = [
        pltpu.make_async_copy(ref.at[head], to, in_sem.at[PLANE + i])
        for i, (ref, to) in enumerate(((wg_ref, wg_held), (wu_ref, wu_held), (wd_ref, wd_held)))
    ]
    for copy in weights:
        copy.start()
    copies = [
        pltpu.make_async_copy(blocks.at[b], held.at[b], in_sem.at[b]) for b in range(PLANE)
    ]
    for copy in copies:
        copy.start()
    for copy in weights:
        copy.wait()
    wg, wu = wg_held[...], wu_held[...]
    wdt = jnp.transpose(wd_held[...])
    for b in range(PLANE):
        copies[b].wait()
        k, vr = held[b, 0], held[b, 1]
        gk = scale_one * dot(k, wg)
        uk = dot(k, wu)
        dh = dot(vr, wdt)
        sig = sigmoid(gk)
        act = gk * sig
        hk = (act * uk).astype(BF)
        dg = (dh * uk * (sig + act * (1.0 - sig))).astype(BF)
        du = (dh * act).astype(BF)
        kt, vt = jnp.transpose(k), jnp.transpose(vr)
        parts = (dot(kt, dg), dot(kt, du), dot(vt, hk))
        for i in range(3):
            if b == 0:
                total[i] = parts[i]
            else:
                total[i] += parts[i]
    both = -scale_one * scale_two
    final[0] = (both * scale_one * total[0]).astype(BF)
    final[1] = (both * total[1]).astype(BF)
    final[2] = (both * total[2]).astype(BF)
    odd = where_ref[4]
    pairs = [(final.at[odd], keep.at[0]), (final.at[2], keep.at[1])]
    each = SENDS // 2
    rows = final.shape[1] // each
    for i in range(each):
        pairs.append((final.at[1 - odd, pl.ds(i * rows, rows)], send[i]))
        pairs.append((final.at[2, pl.ds(i * rows, rows)], send[each + i]))
    run_copies(pairs, sem)


def head_grads(where, blocks, w_gate, w_up, w_down, group, *follows):
    _, size, hidden = w_gate.shape
    tokens = blocks.shape[2]
    return pl.pallas_call(
        functools.partial(grads_kernel, group, size**-0.5, hidden**-0.5),
        out_shape=[jax.ShapeDtypeStruct((2, size, hidden), BF)]
        + [jax.ShapeDtypeStruct((2 * size // SENDS, hidden), BF)] * SENDS,
        in_specs=[SMEM] + [HBM] * 3 + [ANY] * (1 + len(follows)),
        out_specs=[ANY] * (1 + SENDS),
        scratch_shapes=[
            pltpu.VMEM((PLANE, 2, tokens, size), BF),
            pltpu.VMEM((3, size, hidden), F32),
            pltpu.VMEM((3, size, hidden), BF),
            pltpu.VMEM((size, hidden), BF),
            pltpu.VMEM((size, hidden), BF),
            pltpu.VMEM((hidden, size), BF),
            pltpu.SemaphoreType.DMA((PLANE + 3,)),
            pltpu.SemaphoreType.DMA((2 + SENDS,)),
        ],
        compiler_params=pltpu.CompilerParams(vmem_limit_bytes=48 * 1024 * 1024),
        cost_estimate=COST_GRADS,
        name="head_grads",
    )(where, w_gate, w_up, w_down, blocks, *follows)


def combine_kernel(a_ref, *rest):
    parts, out_ref = rest[:SENDS], rest[-1]
    rows = parts[0].shape[0]
    each = out_ref.shape[1] // rows
    for i, part in enumerate(parts):
        at = (i // each, slice(i % each * rows, (i % each + 1) * rows))
        out_ref[at] = (a_ref[at].astype(F32) + part[...].astype(F32)).astype(BF)


def combine(a, parts, *follows):
    return pl.pallas_call(
        combine_kernel,
        out_shape=jax.ShapeDtypeStruct(a.shape, BF),
        in_specs=[VMEM] * (1 + SENDS) + [ANY] * len(follows),
        out_specs=VMEM,
        compiler_params=pltpu.CompilerParams(vmem_limit_bytes=8 * 1024 * 1024),
        cost_estimate=COST_ADD,
        name="add_partials",
    )(a, *parts, *follows)


def newton_kernel(where_ref, mine_ref, other_ref, *rest):
    out_ref, held = rest[-2:]
    size, width = held.shape
    half = size // 2
    mats = []
    for i in range(2):
        grad = mine_ref[i].astype(F32) + other_ref[i].astype(F32)
        norm = jnp.sqrt(jnp.sum(grad * grad))
        mats.append((grad / (norm + 1e-07)).astype(BF))
    for step in range(NS_STEPS):
        squares = [dot(x, x, ((1,), (1,))).astype(BF) for x in mats]
        mixes = [
            (-4.775 * a.astype(F32) + 2.0315 * dot(a, a)).astype(BF) for a in squares
        ]
        nexts = [3.4445 * x.astype(F32) + dot(b, x) for b, x in zip(mixes, mats)]
        if step == NS_STEPS - 1:
            nexts = [n * (0.2 * math.sqrt(width)) for n in nexts]
        mats = [n.astype(BF) for n in nexts]
    out_ref[:size] = mats[0]
    held[...] = mats[1]
    odd = where_ref[4]
    out_ref[size:] = held[pl.ds(pl.multiple_of(odd * half, half), half), :]


def newton(where, mine, other, *follows):
    _, size, hidden = mine.shape
    return pl.pallas_call(
        newton_kernel,
        out_shape=jax.ShapeDtypeStruct((size + size // 2, hidden), BF),
        in_specs=[SMEM] + [VMEM] * 2 + [ANY] * len(follows),
        out_specs=VMEM,
        scratch_shapes=[pltpu.VMEM((size, hidden), BF)],
        compiler_params=pltpu.CompilerParams(vmem_limit_bytes=20 * 1024 * 1024),
        cost_estimate=COST_NEWTON,
        name="newton_schulz",
    )(where, mine, other, *follows)


def run_copies(pairs, sem):
    copies = [pltpu.make_async_copy(a, b, sem.at[i]) for i, (a, b) in enumerate(pairs)]
    for copy in copies:
        copy.start()
    for copy in copies:
        copy.wait()


def place_kernel(count, size, where_ref, *rest):
    blocks, (gate, up, down, sem) = rest[:-4], rest[-4:]
    z, y, x, core = (where_ref[i] for i in range(1, 5))
    half = size // 2

    def put(parity):
        pairs = []
        for i, block in enumerate(blocks):
            group, flip, other, kind = i // 16, i // 8 % 2, i // 4 % 2, i % 4
            side, c = (1 - parity, 1 - core) if other else (parity, core)
            at = ((y, x), (y ^ (1 - c), x ^ c), (y ^ c, x ^ (1 - c)), (1 - y, 1 - x))[kind]
            head = group * PLANE + (lax.rem(z, 2) ^ flip) * 4 + at[0] * 2 + at[1]
            m0 = up if side else gate
            pairs.append((block.at[pl.ds(0, size)], m0.at[head]))
            pairs.append((block.at[pl.ds(size, half)], down.at[head, pl.ds(side * half, half)]))
        run_copies(pairs, sem)

    for parity in range(2):

        @pl.when(core == parity)
        def _():
            put(parity)


def place(where, blocks, shape):
    count = len(blocks)
    return pl.pallas_call(
        functools.partial(place_kernel, count, shape[1]),
        out_shape=[jax.ShapeDtypeStruct(shape, BF)] * 3,
        in_specs=[SMEM] + [ANY] * count,
        out_specs=[ANY] * 3,
        scratch_shapes=[pltpu.SemaphoreType.DMA((2 * count,))],
        compiler_params=pltpu.CompilerParams(vmem_limit_bytes=2 * 1024 * 1024),
        name="place_steps",
    )(where, *blocks)


def permutation(target):
    pairs = []
    for i in range(DEVICES):
        z, y, x, core = target(i // 8, i // 4 % 2, i // 2 % 2, i % 2)
        pairs.append((i, ((z * 2 + y) * 2 + x) * 2 + core))
    return pairs


CUBES = [
    [((2 * zhi + zlo) * 4 + yx) * 2 + core for zlo in range(2) for yx in range(4)]
    for zhi in range(2)
    for core in range(2)
]
Z_MOVES = [permutation(lambda z, y, x, c, s=s: (z ^ s, y, x, c)) for s in range(NZ)]
FIRST_MOVE = permutation(lambda z, y, x, c: (z, y ^ (1 - c), x ^ c, c))
SECOND_MOVE = permutation(lambda z, y, x, c: (z, y ^ c, x ^ (1 - c), c))
CORE_MOVE = permutation(lambda z, y, x, c: (z, y, x, 1 - c))


def move(array, pairs):
    return lax.ppermute(array, "seq", pairs)


def after(array, *others):
    return lax.optimization_barrier((array, *others))[0]


def per_device_fast(queries, keys, values, token_rates, w_gate, w_up, w_down):
    heads, size, hidden = w_gate.shape
    groups = heads // PLANE
    index = lax.axis_index("seq")
    z, core = index // 8, index % 2
    y, x = index // 4 % 2, index // 2 % 2
    where = jnp.stack([z % 2 * 4 + y * 2 + x, z, y, x, core]).astype(jnp.int32)

    packed = [pack_tokens(keys, values, token_rates, 0, size)]
    applied = apply_queries(queries, w_gate, w_up, w_down)
    for group in range(1, groups):
        packed.append(pack_tokens(keys, values, token_rates, group, size, applied))
    received = [
        lax.all_to_all(block, "seq", 0, 0, axis_index_groups=CUBES, tiled=True)
        for block in packed
    ]

    pairs, others, follow = [], [], ()
    for group in range(groups):
        keep, *send = head_grads(where, received[group], w_gate, w_up, w_down, group, *follow)
        pairs.append(combine(keep, [move(block, CORE_MOVE) for block in send], *others[-1:]))
        others.append(move(pairs[-1], Z_MOVES[2]))
        follow = pairs[-1:]
    blocks = []
    for group in range(groups):
        follow = pairs[group + 1 : group + 2]
        block = newton(where, pairs[group], others[group], *follow)
        for flip in range(2):
            if flip:
                block = move(block, Z_MOVES[1])
            one = move(block, FIRST_MOVE)
            two = move(block, SECOND_MOVE)
            three = move(one, SECOND_MOVE)
            mine = [block, one, two, three]
            blocks += mine + [move(b, CORE_MOVE) for b in mine]
    steps = place(where, blocks, w_gate.shape)
    return (applied, *steps)


def solution(mesh):
    in_specs = (
        P("seq", "head"),
        P("seq", "head"),
        P("seq", "head"),
        P("head", "seq"),
        P("head", None, None),
        P("head", None, None),
        P("head", None, None),
    )
    out_specs = (
        P("seq", "head"),
        P("head", None, None),
        P("head", None, None),
        P("head", None, None),
    )
    sizes = mesh.shape

    def per_device(*args):
        heads = args[4].shape[0]
        fast = sizes["seq"] == DEVICES and heads % PLANE == 0
        return (per_device_fast if fast else per_device_plain)(*args)

    return jax.shard_map(
        per_device, mesh=mesh, in_specs=in_specs, out_specs=out_specs, check_vma=False
    )
```

```python
import functools
import math

import jax
import jax.numpy as jnp
from jax import lax
from jax.experimental import pallas as pl
from jax.experimental.pallas import tpu as pltpu
from jax.sharding import PartitionSpec as P

NS_STEPS = 5
BF = jnp.bfloat16
F32 = jnp.float32
VMEM_BYTES = 60 * 1024 * 1024

def cost(us):
    return pl.CostEstimate(flops=1, bytes_accessed=int(us * 3.3e6) + 1, transcendentals=0)


COST_APPLY = cost(0)
COST_PACK = cost(0)
COST_GRADS = cost(0)
COST_ADD = cost(0)
COST_NEWTON = cost(0)
COST_PLACE = cost(0)

HBM = pl.BlockSpec(memory_space=pltpu.HBM)
ANY = pl.BlockSpec(memory_space=pl.ANY)
SMEM = pl.BlockSpec(memory_space=pltpu.SMEM)
VMEM = pl.BlockSpec(memory_space=pltpu.VMEM)

NZ = 4
PLANE = 8
DEVICES = NZ * PLANE


def newton_batch(xmat, width):
    for step in range(NS_STEPS):
        amat = jnp.einsum("mdf,mef->mde", xmat, xmat, preferred_element_type=F32).astype(BF)
        square = jnp.einsum("mde,mef->mdf", amat, amat, preferred_element_type=F32)
        bmat = (-4.775 * amat.astype(F32) + 2.0315 * square).astype(BF)
        nxt = 3.4445 * xmat.astype(F32) + jnp.einsum(
            "mde,mef->mdf", bmat, xmat, preferred_element_type=F32
        )
        if step == NS_STEPS - 1:
            nxt = nxt * (0.2 * math.sqrt(width))
        xmat = nxt.astype(BF)
    return xmat


def per_device_plain(queries, keys, values, token_rates, w_gate, w_up, w_down):
    head_count, head_size, hidden = w_gate.shape
    tokens = queries.shape[0]
    scale_one = head_size ** (-0.5)
    scale_two = hidden ** (-0.5)
    qpart = queries.reshape(tokens, head_count, head_size)
    kpart = keys.reshape(tokens, head_count, head_size)
    vpart = values.reshape(tokens, head_count, head_size)
    gq = scale_one * jnp.einsum("thd,hdf->htf", qpart, w_gate, preferred_element_type=F32)
    uq = scale_one * jnp.einsum("thd,hdf->htf", qpart, w_up, preferred_element_type=F32)
    hq = (jax.nn.silu(gq) * uq).astype(BF)
    applied = (
        scale_two * jnp.einsum("htf,hfd->thd", hq, w_down, preferred_element_type=F32)
    ).astype(BF)
    applied = applied.reshape(tokens, head_count * head_size)
    gk = scale_one * jnp.einsum("thd,hdf->htf", kpart, w_gate, preferred_element_type=F32)
    uk = scale_one * jnp.einsum("thd,hdf->htf", kpart, w_up, preferred_element_type=F32)
    hk = (jax.nn.silu(gk) * uk).astype(BF)
    vrate = (jnp.transpose(token_rates)[:, :, None] * vpart.astype(F32)).astype(BF)
    gdown = -scale_two * jnp.einsum("thd,htf->hdf", vrate, hk, preferred_element_type=F32)
    dhid = -scale_two * jnp.einsum("thd,hfd->htf", vrate, w_down, preferred_element_type=F32)
    sig = jax.nn.sigmoid(gk)
    dgate = (dhid * uk * sig * (1.0 + gk * (1.0 - sig))).astype(BF)
    dup = (dhid * jax.nn.silu(gk)).astype(BF)
    ggate = scale_one * jnp.einsum("thd,htf->hdf", kpart, dgate, preferred_element_type=F32)
    gup = scale_one * jnp.einsum("thd,htf->hdf", kpart, dup, preferred_element_type=F32)
    total = lax.psum(jnp.stack([ggate, gup, gdown], axis=1), "seq")
    norms = jnp.sqrt(jnp.sum(total * total, axis=(2, 3)))
    xmat = (total / (norms[:, :, None, None] + 1e-07)).astype(BF)
    result = newton_batch(xmat.reshape(head_count * 3, head_size, hidden), hidden)
    result = result.reshape(head_count, 3, head_size, hidden)
    return (applied, result[:, 0], result[:, 1], result[:, 2])


def sigmoid(x):
    return 0.5 * jnp.tanh(0.5 * x) + 0.5


def dot(a, b, dims=((1,), (0,))):
    return lax.dot_general(a, b, (dims, ((), ())), preferred_element_type=F32)


def applied_kernel(scale_one, scale_two, q_ref, wg_ref, wu_ref, wd_ref, out_ref):
    heads, size, _ = wg_ref.shape
    for head in range(heads):
        cols = slice(head * size, (head + 1) * size)
        q = q_ref[:, cols]
        gq = scale_one * dot(q, wg_ref[head])
        hq = (gq * sigmoid(gq) * dot(q, wu_ref[head])).astype(BF)
        out_ref[:, cols] = (scale_one * scale_two * dot(hq, wd_ref[head])).astype(BF)


def apply_queries(queries, w_gate, w_up, w_down):
    heads, size, hidden = w_gate.shape
    tokens = queries.shape[0]
    each = 4
    return pl.pallas_call(
        functools.partial(applied_kernel, size**-0.5, hidden**-0.5),
        grid=(heads // each,),
        out_shape=jax.ShapeDtypeStruct(queries.shape, BF),
        in_specs=[
            pl.BlockSpec((tokens, each * size), lambda h: (0, h)),
            pl.BlockSpec((each, size, hidden), lambda h: (h, 0, 0)),
            pl.BlockSpec((each, size, hidden), lambda h: (h, 0, 0)),
            pl.BlockSpec((each, hidden, size), lambda h: (h, 0, 0)),
        ],
        out_specs=pl.BlockSpec((tokens, each * size), lambda h: (0, h)),
        compiler_params=pltpu.CompilerParams(vmem_limit_bytes=VMEM_BYTES),
        cost_estimate=COST_APPLY,
        name="apply_queries",
    )(queries, w_gate, w_up, w_down)


def pack_kernel(size, k_ref, v_ref, rate_ref, *rest):
    out_ref = rest[-1]
    step = pl.program_id(0)
    lanes = lax.broadcasted_iota(jnp.int32, (rate_ref.shape[1], PLANE), 1)
    rates = jnp.transpose(rate_ref[...])
    for i in range(out_ref.shape[0]):
        cols = slice(i * size, (i + 1) * size)
        here = lanes == step * out_ref.shape[0] + i
        rate = jnp.sum(jnp.where(here, rates, 0.0), axis=1, keepdims=True)
        out_ref[i, 0] = k_ref[:, cols]
        out_ref[i, 1] = (rate * v_ref[:, cols].astype(F32)).astype(BF)


def pack_tokens(keys, values, rates, group, size, *follows):
    tokens = keys.shape[0]
    each = 4
    steps = PLANE // each
    return pl.pallas_call(
        functools.partial(pack_kernel, size),
        grid=(steps,),
        out_shape=jax.ShapeDtypeStruct((PLANE, 2, tokens, size), BF),
        in_specs=[
            pl.BlockSpec((tokens, each * size), lambda i: (0, group * steps + i)),
            pl.BlockSpec((tokens, each * size), lambda i: (0, group * steps + i)),
            pl.BlockSpec((PLANE, tokens), lambda i: (group, 0)),
        ]
        + [ANY] * len(follows),
        out_specs=pl.BlockSpec((each, 2, tokens, size), lambda i: (i, 0, 0, 0)),
        compiler_params=pltpu.CompilerParams(vmem_limit_bytes=VMEM_BYTES),
        cost_estimate=COST_PACK,
        name="pack_tokens",
    )(keys, values, rates, *follows)


def grads_kernel(group, scale_one, scale_two, where_ref, wg_ref, wu_ref, wd_ref, blocks, *rest):
    keep, *send = rest[-12:-8]
    held, total, final, wg_held, wu_held, wd_held, in_sem, sem = rest[-8:]
    head = group * PLANE + where_ref[0]
    weights = [
        pltpu.make_async_copy(ref.at[head], to, in_sem.at[PLANE + i])
        for i, (ref, to) in enumerate(((wg_ref, wg_held), (wu_ref, wu_held), (wd_ref, wd_held)))
    ]
    for copy in weights:
        copy.start()
    tokens = held.shape[1] // PLANE
    copies = [
        pltpu.make_async_copy(blocks.at[b], held.at[:, pl.ds(b * tokens, tokens)], in_sem.at[b])
        for b in range(PLANE)
    ]
    for copy in copies:
        copy.start()
    for copy in weights:
        copy.wait()
    wg, wu = wg_held[...], wu_held[...]
    wdt = jnp.transpose(wd_held[...])
    for b in range(0, PLANE, 2):
        copies[b].wait()
        copies[b + 1].wait()
        rows = slice(b * tokens, (b + 2) * tokens)
        k, vr = held[0, rows], held[1, rows]
        gk = scale_one * dot(k, wg)
        uk = dot(k, wu)
        dh = dot(vr, wdt)
        sig = sigmoid(gk)
        act = gk * sig
        hk = (act * uk).astype(BF)
        dg = (dh * uk * (sig + act * (1.0 - sig))).astype(BF)
        du = (dh * act).astype(BF)
        kt, vt = jnp.transpose(k), jnp.transpose(vr)
        parts = (dot(kt, dg), dot(kt, du), dot(vt, hk))
        for i in range(3):
            if b == 0:
                total[i] = parts[i]
            else:
                total[i] += parts[i]
    both = -scale_one * scale_two
    final[0] = (both * scale_one * total[0]).astype(BF)
    final[1] = (both * total[1]).astype(BF)
    final[2] = (both * total[2]).astype(BF)
    core, half = where_ref[4], final.shape[1] // 2
    mine = pl.ds(pl.multiple_of(core * half, half), half)
    others = pl.ds(pl.multiple_of((1 - core) * half, half), half)
    run_copies(
        [
            (final.at[1 - core, pl.ds(0, half)], send[0]),
            (final.at[1 - core, pl.ds(half, half)], send[1]),
            (final.at[2, others], send[2]),
            (final.at[core], keep.at[pl.ds(0, 2 * half)]),
            (final.at[2, mine], keep.at[pl.ds(2 * half, half)]),
        ],
        sem,
    )


def head_grads(where, blocks, w_gate, w_up, w_down, group, *follows):
    _, size, hidden = w_gate.shape
    tokens = blocks.shape[2]
    return pl.pallas_call(
        functools.partial(grads_kernel, group, size**-0.5, hidden**-0.5),
        out_shape=[jax.ShapeDtypeStruct((size + size // 2, hidden), BF)]
        + [jax.ShapeDtypeStruct((size // 2, hidden), BF)] * 3,
        in_specs=[SMEM] + [HBM] * 3 + [ANY] * (1 + len(follows)),
        out_specs=[ANY] * 4,
        scratch_shapes=[
            pltpu.VMEM((2, PLANE * tokens, size), BF),
            pltpu.VMEM((3, size, hidden), F32),
            pltpu.VMEM((3, size, hidden), BF),
            pltpu.VMEM((size, hidden), BF),
            pltpu.VMEM((size, hidden), BF),
            pltpu.VMEM((hidden, size), BF),
            pltpu.SemaphoreType.DMA((PLANE + 3,)),
            pltpu.SemaphoreType.DMA((5,)),
        ],
        compiler_params=pltpu.CompilerParams(vmem_limit_bytes=48 * 1024 * 1024),
        cost_estimate=COST_GRADS,
        name="head_grads",
    )(where, w_gate, w_up, w_down, blocks, *follows)


def combine_kernel(keep_ref, a_ref, b_ref, c_ref, *rest):
    out_ref, part_ref = rest[-2:]
    rows = part_ref.shape[0]
    for i, ref in enumerate((a_ref, b_ref, c_ref)):
        at = slice(i * rows, (i + 1) * rows)
        total = (keep_ref[at].astype(F32) + ref[...].astype(F32)).astype(BF)
        out_ref[at] = total
    part_ref[...] = total


def combine(keep, parts, *follows):
    return pl.pallas_call(
        combine_kernel,
        out_shape=[
            jax.ShapeDtypeStruct(keep.shape, BF),
            jax.ShapeDtypeStruct(parts[-1].shape, BF),
        ],
        in_specs=[VMEM] * 4 + [ANY] * len(follows),
        out_specs=[VMEM] * 2,
        compiler_params=pltpu.CompilerParams(vmem_limit_bytes=8 * 1024 * 1024),
        cost_estimate=COST_ADD,
        name="add_partials",
    )(keep, *parts, *follows)


def newton_kernel(where_ref, *rest):
    mine_ref, other_ref, mine_sib, other_sib = rest[:4]
    out_ref, total, held = rest[-3:]
    size, width = held.shape
    half = size // 2
    core = where_ref[4]
    mine = pl.ds(pl.multiple_of(core * half, half), half)
    others = pl.ds(pl.multiple_of((1 - core) * half, half), half)
    total[mine, :] = mine_ref[size:].astype(F32) + other_ref[size:].astype(F32)
    total[others, :] = mine_sib[...].astype(F32) + other_sib[...].astype(F32)
    mats = []
    main = mine_ref[:size].astype(F32) + other_ref[:size].astype(F32)
    for grad in (main, total[...]):
        norm = jnp.sqrt(jnp.sum(grad * grad))
        mats.append((grad / (norm + 1e-07)).astype(BF))
    for step in range(NS_STEPS):
        squares = [dot(x, x, ((1,), (1,))).astype(BF) for x in mats]
        mixes = [
            (-4.775 * a.astype(F32) + 2.0315 * dot(a, a)).astype(BF) for a in squares
        ]
        nexts = [3.4445 * x.astype(F32) + dot(b, x) for b, x in zip(mixes, mats)]
        if step == NS_STEPS - 1:
            nexts = [n * (0.2 * math.sqrt(width)) for n in nexts]
        mats = [n.astype(BF) for n in nexts]
    out_ref[:size] = mats[0]
    held[...] = mats[1]
    out_ref[size:] = held[mine, :]


def newton(where, parts, *follows):
    rows, hidden = parts[0].shape
    size = rows * 2 // 3
    return pl.pallas_call(
        newton_kernel,
        out_shape=jax.ShapeDtypeStruct((rows, hidden), BF),
        in_specs=[SMEM] + [VMEM] * len(parts) + [ANY] * len(follows),
        out_specs=VMEM,
        scratch_shapes=[pltpu.VMEM((size, hidden), F32), pltpu.VMEM((size, hidden), BF)],
        compiler_params=pltpu.CompilerParams(vmem_limit_bytes=20 * 1024 * 1024),
        cost_estimate=COST_NEWTON,
        name="newton_schulz",
    )(where, *parts, *follows)


def run_copies(pairs, sem):
    copies = [pltpu.make_async_copy(a, b, sem.at[i]) for i, (a, b) in enumerate(pairs)]
    for copy in copies:
        copy.start()
    for copy in copies:
        copy.wait()


def place_kernel(group, which, size, where_ref, *rest):
    blocks, (gate, up, down, sem) = rest[: len(which)], rest[-4:]
    z, y, x, core = (where_ref[i] for i in range(1, 5))
    half = size // 2

    def put(parity):
        pairs = []
        for i, block in zip(which, blocks):
            flip, other, kind = i // 8, i // 4 % 2, i % 4
            side, c = (1 - parity, 1 - core) if other else (parity, core)
            at = ((y, x), (y ^ (1 - c), x ^ c), (y ^ c, x ^ (1 - c)), (1 - y, 1 - x))[kind]
            head = group * PLANE + (lax.rem(z, 2) ^ flip) * 4 + at[0] * 2 + at[1]
            m0 = up if side else gate
            pairs.append((block.at[pl.ds(0, size)], m0.at[head]))
            pairs.append((block.at[pl.ds(size, half)], down.at[head, pl.ds(side * half, half)]))
        run_copies(pairs, sem)

    for parity in range(2):

        @pl.when(core == parity)
        def _():
            put(parity)


def place(where, blocks, steps, shape, group, which=tuple(range(16))):
    count = len(blocks)
    return pl.pallas_call(
        functools.partial(place_kernel, group, which, shape[1]),
        out_shape=[jax.ShapeDtypeStruct(shape, BF)] * 3,
        in_specs=[SMEM] + [VMEM] * count + [ANY] * len(steps),
        out_specs=[ANY] * 3,
        scratch_shapes=[pltpu.SemaphoreType.DMA((2 * count,))],
        input_output_aliases={1 + count + i: i for i in range(len(steps))},
        compiler_params=pltpu.CompilerParams(vmem_limit_bytes=16 * 1024 * 1024),
        cost_estimate=COST_PLACE,
        name="place_steps",
    )(where, *blocks, *steps)


def permutation(target):
    pairs = []
    for i in range(DEVICES):
        z, y, x, core = target(i // 8, i // 4 % 2, i // 2 % 2, i % 2)
        pairs.append((i, ((z * 2 + y) * 2 + x) * 2 + core))
    return pairs


CUBES = [
    [((2 * zhi + zlo) * 4 + yx) * 2 + core for zlo in range(2) for yx in range(4)]
    for zhi in range(2)
    for core in range(2)
]
Z_MOVES = [permutation(lambda z, y, x, c, s=s: (z ^ s, y, x, c)) for s in range(NZ)]
FIRST_MOVE = permutation(lambda z, y, x, c: (z, y ^ (1 - c), x ^ c, c))
SECOND_MOVE = permutation(lambda z, y, x, c: (z, y ^ c, x ^ (1 - c), c))
CORE_MOVE = permutation(lambda z, y, x, c: (z, y, x, 1 - c))


def move(array, pairs):
    return lax.ppermute(array, "seq", pairs)


def after(array, *others):
    return lax.optimization_barrier((array, *others))[0]


def per_device_fast(queries, keys, values, token_rates, w_gate, w_up, w_down):
    heads, size, hidden = w_gate.shape
    groups = heads // PLANE
    index = lax.axis_index("seq")
    z, core = index // 8, index % 2
    y, x = index // 4 % 2, index // 2 % 2
    where = jnp.stack([z % 2 * 4 + y * 2 + x, z, y, x, core]).astype(jnp.int32)

    packed = [pack_tokens(keys, values, token_rates, 0, size)]
    applied = apply_queries(queries, w_gate, w_up, w_down)
    for group in range(1, groups):
        packed.append(pack_tokens(keys, values, token_rates, group, size, applied))
    received = [
        lax.all_to_all(block, "seq", 0, 0, axis_index_groups=CUBES, tiled=True)
        for block in packed
    ]

    def summed(group, waits, *follow):
        keep, *send = head_grads(where, received[group], w_gate, w_up, w_down, group, *follow)
        return combine(keep, [move(block, CORE_MOVE) for block in send], *waits)

    def round_two(one, two, far):
        return move(one, Z_MOVES[1]), move(two, FIRST_MOVE), move(far, SECOND_MOVE)

    def with_sibling(*gathered):
        return [*gathered] + [move(block, CORE_MOVE) for block in gathered]

    mine, part = summed(0, ())
    other = move(mine, Z_MOVES[2])
    parts = (mine, other, move(part, CORE_MOVE), move(other[size:], CORE_MOVE))
    mine_b, part_b = summed(1, (other,), mine)
    other_b = move(mine_b, Z_MOVES[2])
    near = newton(where, parts, mine_b)
    one, two, far = (move(near, to) for to in (FIRST_MOVE, SECOND_MOVE, Z_MOVES[1]))
    one, two, far, other_b = lax.optimization_barrier((one, two, far, other_b))
    far_one, three, far_two = round_two(one, two, far)
    parts = (mine_b, other_b, move(part_b, CORE_MOVE), move(other_b[size:], CORE_MOVE))
    near_b = newton(where, parts)
    near_b, three, far_two = lax.optimization_barrier((near_b, three, far_two))
    far_three = move(far_one, SECOND_MOVE)
    one_b, two_b, far_b = (move(near_b, to) for to in (FIRST_MOVE, SECOND_MOVE, Z_MOVES[1]))
    blocks = with_sibling(near, one, two, three)
    one, two, far_b, far_three = lax.optimization_barrier((one_b, two_b, far_b, far_three))
    blocks += with_sibling(far, far_one, far_two, far_three)
    steps = place(where, blocks, (), w_gate.shape, 0)
    far_one, three, far_two = round_two(one, two, far_b)
    far_one, three, far_two = lax.optimization_barrier((far_one, three, far_two))
    far_three = move(far_one, SECOND_MOVE)
    blocks = with_sibling(near_b, one, two, three) + with_sibling(far_b, far_one, far_two)
    which = (*range(11), 12, 13, 14)
    steps = place(where, blocks, steps, w_gate.shape, 1, which)
    far_three, *steps = lax.optimization_barrier((far_three, *steps))
    steps = place(where, with_sibling(far_three), steps, w_gate.shape, 1, (11, 15))
    return (applied, *steps)


def solution(mesh):
    in_specs = (
        P("seq", "head"),
        P("seq", "head"),
        P("seq", "head"),
        P("head", "seq"),
        P("head", None, None),
        P("head", None, None),
        P("head", None, None),
    )
    out_specs = (
        P("seq", "head"),
        P("head", None, None),
        P("head", None, None),
        P("head", None, None),
    )
    sizes = mesh.shape

    def per_device(*args):
        heads = args[4].shape[0]
        fast = sizes["seq"] == DEVICES and heads == 2 * PLANE
        return (per_device_fast if fast else per_device_plain)(*args)

    return jax.shard_map(
        per_device, mesh=mesh, in_specs=in_specs, out_specs=out_specs, check_vma=False
    )
```

```python
import functools
import math

import jax
import jax.numpy as jnp
from jax import lax
from jax.experimental import pallas as pl
from jax.experimental.pallas import tpu as pltpu
from jax.sharding import PartitionSpec as P

NS_STEPS = 5
BF = jnp.bfloat16
F32 = jnp.float32
VMEM_BYTES = 60 * 1024 * 1024

def cost(us):
    return pl.CostEstimate(flops=1, bytes_accessed=int(us * 3.3e6) + 1, transcendentals=0)


COST_APPLY = cost(0)
COST_PACK = cost(0)
COST_GRADS = cost(0)
COST_ADD = cost(0)
COST_NEWTON = cost(0)
COST_PLACE = cost(0)

HBM = pl.BlockSpec(memory_space=pltpu.HBM)
ANY = pl.BlockSpec(memory_space=pl.ANY)
SMEM = pl.BlockSpec(memory_space=pltpu.SMEM)
VMEM = pl.BlockSpec(memory_space=pltpu.VMEM)

NZ = 4
PLANE = 8
DEVICES = NZ * PLANE


def newton_batch(xmat, width):
    for step in range(NS_STEPS):
        amat = jnp.einsum("mdf,mef->mde", xmat, xmat, preferred_element_type=F32).astype(BF)
        square = jnp.einsum("mde,mef->mdf", amat, amat, preferred_element_type=F32)
        bmat = (-4.775 * amat.astype(F32) + 2.0315 * square).astype(BF)
        nxt = 3.4445 * xmat.astype(F32) + jnp.einsum(
            "mde,mef->mdf", bmat, xmat, preferred_element_type=F32
        )
        if step == NS_STEPS - 1:
            nxt = nxt * (0.2 * math.sqrt(width))
        xmat = nxt.astype(BF)
    return xmat


def per_device_plain(queries, keys, values, token_rates, w_gate, w_up, w_down):
    head_count, head_size, hidden = w_gate.shape
    tokens = queries.shape[0]
    scale_one = head_size ** (-0.5)
    scale_two = hidden ** (-0.5)
    qpart = queries.reshape(tokens, head_count, head_size)
    kpart = keys.reshape(tokens, head_count, head_size)
    vpart = values.reshape(tokens, head_count, head_size)
    gq = scale_one * jnp.einsum("thd,hdf->htf", qpart, w_gate, preferred_element_type=F32)
    uq = scale_one * jnp.einsum("thd,hdf->htf", qpart, w_up, preferred_element_type=F32)
    hq = (jax.nn.silu(gq) * uq).astype(BF)
    applied = (
        scale_two * jnp.einsum("htf,hfd->thd", hq, w_down, preferred_element_type=F32)
    ).astype(BF)
    applied = applied.reshape(tokens, head_count * head_size)
    gk = scale_one * jnp.einsum("thd,hdf->htf", kpart, w_gate, preferred_element_type=F32)
    uk = scale_one * jnp.einsum("thd,hdf->htf", kpart, w_up, preferred_element_type=F32)
    hk = (jax.nn.silu(gk) * uk).astype(BF)
    vrate = (jnp.transpose(token_rates)[:, :, None] * vpart.astype(F32)).astype(BF)
    gdown = -scale_two * jnp.einsum("thd,htf->hdf", vrate, hk, preferred_element_type=F32)
    dhid = -scale_two * jnp.einsum("thd,hfd->htf", vrate, w_down, preferred_element_type=F32)
    sig = jax.nn.sigmoid(gk)
    dgate = (dhid * uk * sig * (1.0 + gk * (1.0 - sig))).astype(BF)
    dup = (dhid * jax.nn.silu(gk)).astype(BF)
    ggate = scale_one * jnp.einsum("thd,htf->hdf", kpart, dgate, preferred_element_type=F32)
    gup = scale_one * jnp.einsum("thd,htf->hdf", kpart, dup, preferred_element_type=F32)
    total = lax.psum(jnp.stack([ggate, gup, gdown], axis=1), "seq")
    norms = jnp.sqrt(jnp.sum(total * total, axis=(2, 3)))
    xmat = (total / (norms[:, :, None, None] + 1e-07)).astype(BF)
    result = newton_batch(xmat.reshape(head_count * 3, head_size, hidden), hidden)
    result = result.reshape(head_count, 3, head_size, hidden)
    return (applied, result[:, 0], result[:, 1], result[:, 2])


def sigmoid(x):
    return 0.5 * jnp.tanh(0.5 * x) + 0.5


def dot(a, b, dims=((1,), (0,))):
    return lax.dot_general(a, b, (dims, ((), ())), preferred_element_type=F32)


def applied_kernel(scale_one, scale_two, q_ref, wg_ref, wu_ref, wd_ref, out_ref):
    heads, size, _ = wg_ref.shape
    for head in range(heads):
        cols = slice(head * size, (head + 1) * size)
        q = q_ref[:, cols]
        gq = scale_one * dot(q, wg_ref[head])
        hq = (gq * sigmoid(gq) * dot(q, wu_ref[head])).astype(BF)
        out_ref[:, cols] = (scale_one * scale_two * dot(hq, wd_ref[head])).astype(BF)


def apply_queries(queries, w_gate, w_up, w_down):
    heads, size, hidden = w_gate.shape
    tokens = queries.shape[0]
    each = 4
    return pl.pallas_call(
        functools.partial(applied_kernel, size**-0.5, hidden**-0.5),
        grid=(heads // each,),
        out_shape=jax.ShapeDtypeStruct(queries.shape, BF),
        in_specs=[
            pl.BlockSpec((tokens, each * size), lambda h: (0, h)),
            pl.BlockSpec((each, size, hidden), lambda h: (h, 0, 0)),
            pl.BlockSpec((each, size, hidden), lambda h: (h, 0, 0)),
            pl.BlockSpec((each, hidden, size), lambda h: (h, 0, 0)),
        ],
        out_specs=pl.BlockSpec((tokens, each * size), lambda h: (0, h)),
        compiler_params=pltpu.CompilerParams(vmem_limit_bytes=VMEM_BYTES),
        cost_estimate=COST_APPLY,
        name="apply_queries",
    )(queries, w_gate, w_up, w_down)


def pack_kernel(size, k_ref, v_ref, rate_ref, *rest):
    out_ref = rest[-1]
    step = pl.program_id(0)
    lanes = lax.broadcasted_iota(jnp.int32, (rate_ref.shape[1], PLANE), 1)
    rates = jnp.transpose(rate_ref[...])
    for i in range(out_ref.shape[0]):
        cols = slice(i * size, (i + 1) * size)
        here = lanes == step * out_ref.shape[0] + i
        rate = jnp.sum(jnp.where(here, rates, 0.0), axis=1, keepdims=True)
        out_ref[i, 0] = k_ref[:, cols]
        out_ref[i, 1] = (rate * v_ref[:, cols].astype(F32)).astype(BF)


def pack_tokens(keys, values, rates, group, size, *follows):
    tokens = keys.shape[0]
    each = 4
    steps = PLANE // each
    return pl.pallas_call(
        functools.partial(pack_kernel, size),
        grid=(steps,),
        out_shape=jax.ShapeDtypeStruct((PLANE, 2, tokens, size), BF),
        in_specs=[
            pl.BlockSpec((tokens, each * size), lambda i: (0, group * steps + i)),
            pl.BlockSpec((tokens, each * size), lambda i: (0, group * steps + i)),
            pl.BlockSpec((PLANE, tokens), lambda i: (group, 0)),
        ]
        + [ANY] * len(follows),
        out_specs=pl.BlockSpec((each, 2, tokens, size), lambda i: (i, 0, 0, 0)),
        compiler_params=pltpu.CompilerParams(vmem_limit_bytes=VMEM_BYTES),
        cost_estimate=COST_PACK,
        name="pack_tokens",
    )(keys, values, rates, *follows)


def grads_kernel(group, scale_one, scale_two, where_ref, wg_ref, wu_ref, wd_ref, blocks, *rest):
    keep, *send = rest[-12:-8]
    held, total, final, wg_held, wu_held, wd_held, in_sem, sem = rest[-8:]
    head = group * PLANE + where_ref[0]
    weights = [
        pltpu.make_async_copy(ref.at[head], to, in_sem.at[PLANE + i])
        for i, (ref, to) in enumerate(((wg_ref, wg_held), (wu_ref, wu_held), (wd_ref, wd_held)))
    ]
    for copy in weights:
        copy.start()
    tokens = held.shape[1] // PLANE
    copies = [
        pltpu.make_async_copy(blocks.at[b], held.at[:, pl.ds(b * tokens, tokens)], in_sem.at[b])
        for b in range(PLANE)
    ]
    for copy in copies:
        copy.start()
    for copy in weights:
        copy.wait()
    wg, wu = wg_held[...], wu_held[...]
    wdt = jnp.transpose(wd_held[...])
    for b in range(0, PLANE, 2):
        copies[b].wait()
        copies[b + 1].wait()
        rows = slice(b * tokens, (b + 2) * tokens)
        k, vr = held[0, rows], held[1, rows]
        gk = scale_one * dot(k, wg)
        uk = dot(k, wu)
        dh = dot(vr, wdt)
        sig = sigmoid(gk)
        act = gk * sig
        hk = (act * uk).astype(BF)
        dg = (dh * uk * (sig + act * (1.0 - sig))).astype(BF)
        du = (dh * act).astype(BF)
        kt, vt = jnp.transpose(k), jnp.transpose(vr)
        parts = (dot(kt, dg), dot(kt, du), dot(vt, hk))
        for i in range(3):
            if b == 0:
                total[i] = parts[i]
            else:
                total[i] += parts[i]
    both = -scale_one * scale_two
    final[0] = (both * scale_one * total[0]).astype(BF)
    final[1] = (both * total[1]).astype(BF)
    final[2] = (both * total[2]).astype(BF)
    core, half = where_ref[4], final.shape[1] // 2
    mine = pl.ds(pl.multiple_of(core * half, half), half)
    others = pl.ds(pl.multiple_of((1 - core) * half, half), half)
    run_copies(
        [
            (final.at[1 - core, pl.ds(0, half)], send[0]),
            (final.at[1 - core, pl.ds(half, half)], send[1]),
            (final.at[2, others], send[2]),
            (final.at[core], keep.at[pl.ds(0, 2 * half)]),
            (final.at[2, mine], keep.at[pl.ds(2 * half, half)]),
        ],
        sem,
    )


def head_grads(where, blocks, w_gate, w_up, w_down, group, *follows):
    _, size, hidden = w_gate.shape
    tokens = blocks.shape[2]
    return pl.pallas_call(
        functools.partial(grads_kernel, group, size**-0.5, hidden**-0.5),
        out_shape=[jax.ShapeDtypeStruct((size + size // 2, hidden), BF)]
        + [jax.ShapeDtypeStruct((size // 2, hidden), BF)] * 3,
        in_specs=[SMEM] + [HBM] * 3 + [ANY] * (1 + len(follows)),
        out_specs=[ANY] * 4,
        scratch_shapes=[
            pltpu.VMEM((2, PLANE * tokens, size), BF),
            pltpu.VMEM((3, size, hidden), F32),
            pltpu.VMEM((3, size, hidden), BF),
            pltpu.VMEM((size, hidden), BF),
            pltpu.VMEM((size, hidden), BF),
            pltpu.VMEM((hidden, size), BF),
            pltpu.SemaphoreType.DMA((PLANE + 3,)),
            pltpu.SemaphoreType.DMA((5,)),
        ],
        compiler_params=pltpu.CompilerParams(vmem_limit_bytes=48 * 1024 * 1024),
        cost_estimate=COST_GRADS,
        name="head_grads",
    )(where, w_gate, w_up, w_down, blocks, *follows)


def combine_kernel(keep_ref, a_ref, b_ref, c_ref, *rest):
    out_ref, part_ref = rest[-2:]
    rows = part_ref.shape[0]
    for i, ref in enumerate((a_ref, b_ref, c_ref)):
        at = slice(i * rows, (i + 1) * rows)
        total = (keep_ref[at].astype(F32) + ref[...].astype(F32)).astype(BF)
        out_ref[at] = total
    part_ref[...] = total


def combine(keep, parts, *follows):
    return pl.pallas_call(
        combine_kernel,
        out_shape=[
            jax.ShapeDtypeStruct(keep.shape, BF),
            jax.ShapeDtypeStruct(parts[-1].shape, BF),
        ],
        in_specs=[VMEM] * 4 + [ANY] * len(follows),
        out_specs=[VMEM] * 2,
        compiler_params=pltpu.CompilerParams(vmem_limit_bytes=8 * 1024 * 1024),
        cost_estimate=COST_ADD,
        name="add_partials",
    )(keep, *parts, *follows)


def newton_kernel(where_ref, *rest):
    mine_ref, other_ref, mine_sib, other_sib = rest[:4]
    out_ref, total, held = rest[-3:]
    size, width = held.shape
    half = size // 2
    core = where_ref[4]
    mine = pl.ds(pl.multiple_of(core * half, half), half)
    others = pl.ds(pl.multiple_of((1 - core) * half, half), half)
    total[mine, :] = mine_ref[size:].astype(F32) + other_ref[size:].astype(F32)
    total[others, :] = mine_sib[...].astype(F32) + other_sib[...].astype(F32)
    mats = []
    main = mine_ref[:size].astype(F32) + other_ref[:size].astype(F32)
    for grad in (main, total[...]):
        norm = jnp.sqrt(jnp.sum(grad * grad))
        mats.append((grad / (norm + 1e-07)).astype(BF))
    for step in range(NS_STEPS):
        squares = [dot(x, x, ((1,), (1,))).astype(BF) for x in mats]
        mixes = [
            (-4.775 * a.astype(F32) + 2.0315 * dot(a, a)).astype(BF) for a in squares
        ]
        nexts = [3.4445 * x.astype(F32) + dot(b, x) for b, x in zip(mixes, mats)]
        if step == NS_STEPS - 1:
            nexts = [n * (0.2 * math.sqrt(width)) for n in nexts]
        mats = [n.astype(BF) for n in nexts]
    out_ref[:size] = mats[0]
    held[...] = mats[1]
    out_ref[size:] = held[mine, :]


def newton(where, parts, *follows):
    rows, hidden = parts[0].shape
    size = rows * 2 // 3
    return pl.pallas_call(
        newton_kernel,
        out_shape=jax.ShapeDtypeStruct((rows, hidden), BF),
        in_specs=[SMEM] + [VMEM] * len(parts) + [ANY] * len(follows),
        out_specs=VMEM,
        scratch_shapes=[pltpu.VMEM((size, hidden), F32), pltpu.VMEM((size, hidden), BF)],
        compiler_params=pltpu.CompilerParams(vmem_limit_bytes=20 * 1024 * 1024),
        cost_estimate=COST_NEWTON,
        name="newton_schulz",
    )(where, *parts, *follows)


def run_copies(pairs, sem):
    copies = [pltpu.make_async_copy(a, b, sem.at[i]) for i, (a, b) in enumerate(pairs)]
    for copy in copies:
        copy.start()
    for copy in copies:
        copy.wait()


def place_kernel(group, which, size, where_ref, *rest):
    blocks, (gate, up, down, sem) = rest[: len(which)], rest[-4:]
    z, y, x, core = (where_ref[i] for i in range(1, 5))
    half = size // 2

    def put(parity):
        pairs = []
        for i, block in zip(which, blocks):
            flip, other, kind = i // 8, i // 4 % 2, i % 4
            side, c = (1 - parity, 1 - core) if other else (parity, core)
            at = ((y, x), (y ^ (1 - c), x ^ c), (y ^ c, x ^ (1 - c)), (1 - y, 1 - x))[kind]
            head = group * PLANE + (lax.rem(z, 2) ^ flip) * 4 + at[0] * 2 + at[1]
            m0 = up if side else gate
            pairs.append((block.at[pl.ds(0, size)], m0.at[head]))
            pairs.append((block.at[pl.ds(size, half)], down.at[head, pl.ds(side * half, half)]))
        run_copies(pairs, sem)

    for parity in range(2):

        @pl.when(core == parity)
        def _():
            put(parity)


def place(where, blocks, steps, shape, group, which=tuple(range(16))):
    count = len(blocks)
    return pl.pallas_call(
        functools.partial(place_kernel, group, which, shape[1]),
        out_shape=[jax.ShapeDtypeStruct(shape, BF)] * 3,
        in_specs=[SMEM] + [VMEM] * count + [ANY] * len(steps),
        out_specs=[ANY] * 3,
        scratch_shapes=[pltpu.SemaphoreType.DMA((2 * count,))],
        input_output_aliases={1 + count + i: i for i in range(len(steps))},
        compiler_params=pltpu.CompilerParams(vmem_limit_bytes=16 * 1024 * 1024),
        cost_estimate=COST_PLACE,
        name="place_steps",
    )(where, *blocks, *steps)


def permutation(target):
    pairs = []
    for i in range(DEVICES):
        z, y, x, core = target(i // 8, i // 4 % 2, i // 2 % 2, i % 2)
        pairs.append((i, ((z * 2 + y) * 2 + x) * 2 + core))
    return pairs


CUBES = [
    [((2 * zhi + zlo) * 4 + yx) * 2 + core for zlo in range(2) for yx in range(4)]
    for zhi in range(2)
    for core in range(2)
]
Z_MOVES = [permutation(lambda z, y, x, c, s=s: (z ^ s, y, x, c)) for s in range(NZ)]
FIRST_MOVE = permutation(lambda z, y, x, c: (z, y ^ (1 - c), x ^ c, c))
SECOND_MOVE = permutation(lambda z, y, x, c: (z, y ^ c, x ^ (1 - c), c))
CORE_MOVE = permutation(lambda z, y, x, c: (z, y, x, 1 - c))


def move(array, pairs):
    return lax.ppermute(array, "seq", pairs)


def after(array, *others):
    return lax.optimization_barrier((array, *others))[0]


def per_device_fast(queries, keys, values, token_rates, w_gate, w_up, w_down):
    heads, size, hidden = w_gate.shape
    groups = heads // PLANE
    index = lax.axis_index("seq")
    z, core = index // 8, index % 2
    y, x = index // 4 % 2, index // 2 % 2
    where = jnp.stack([z % 2 * 4 + y * 2 + x, z, y, x, core]).astype(jnp.int32)

    packed = [pack_tokens(keys, values, token_rates, 0, size)]
    applied = apply_queries(queries, w_gate, w_up, w_down)
    for group in range(1, groups):
        packed.append(pack_tokens(keys, values, token_rates, group, size, applied))
    received = [
        lax.all_to_all(block, "seq", 0, 0, axis_index_groups=CUBES, tiled=True)
        for block in packed
    ]

    def summed(group, waits, *follow):
        keep, *send = head_grads(where, received[group], w_gate, w_up, w_down, group, *follow)
        return combine(keep, [move(block, CORE_MOVE) for block in send], *waits)

    def round_two(one, two, far):
        return move(one, Z_MOVES[1]), move(two, FIRST_MOVE), move(far, SECOND_MOVE)

    def with_sibling(*gathered):
        return [*gathered] + [move(block, CORE_MOVE) for block in gathered]

    mine, part = summed(0, ())
    other = move(mine, Z_MOVES[2])
    parts = (mine, other, move(part, CORE_MOVE), move(other[size:], CORE_MOVE))
    mine_b, part_b = summed(1, (other,), mine)
    other_b = move(mine_b, Z_MOVES[2])
    near = newton(where, parts, mine_b)
    one, two, far = (move(near, to) for to in (FIRST_MOVE, SECOND_MOVE, Z_MOVES[1]))
    one, two, other_b = lax.optimization_barrier((one, two, other_b))
    far_one, three = move(one, Z_MOVES[1]), move(two, FIRST_MOVE)
    parts = (mine_b, other_b, move(part_b, CORE_MOVE), move(other_b[size:], CORE_MOVE))
    near_b = newton(where, parts)
    near_b, three, far = lax.optimization_barrier((near_b, three, far))
    far_two = move(far, SECOND_MOVE)
    far_three = move(far_one, SECOND_MOVE)
    one_b, two_b, far_b = (move(near_b, to) for to in (FIRST_MOVE, SECOND_MOVE, Z_MOVES[1]))
    blocks = with_sibling(near, one, two, three)
    one, two, far_b, far_two, far_three = lax.optimization_barrier(
        (one_b, two_b, far_b, far_two, far_three)
    )
    blocks += with_sibling(far, far_one, far_two, far_three)
    steps = place(where, blocks, (), w_gate.shape, 0)
    far_one, three, far_two = round_two(one, two, far_b)
    far_one, three, far_two = lax.optimization_barrier((far_one, three, far_two))
    far_three = move(far_one, SECOND_MOVE)
    blocks = with_sibling(near_b, one, two, three) + with_sibling(far_b, far_one, far_two)
    which = (*range(11), 12, 13, 14)
    steps = place(where, blocks, steps, w_gate.shape, 1, which)
    far_three, *steps = lax.optimization_barrier((far_three, *steps))
    steps = place(where, with_sibling(far_three), steps, w_gate.shape, 1, (11, 15))
    return (applied, *steps)


def solution(mesh):
    in_specs = (
        P("seq", "head"),
        P("seq", "head"),
        P("seq", "head"),
        P("head", "seq"),
        P("head", None, None),
        P("head", None, None),
        P("head", None, None),
    )
    out_specs = (
        P("seq", "head"),
        P("head", None, None),
        P("head", None, None),
        P("head", None, None),
    )
    sizes = mesh.shape

    def per_device(*args):
        heads = args[4].shape[0]
        fast = sizes["seq"] == DEVICES and heads == 2 * PLANE
        return (per_device_fast if fast else per_device_plain)(*args)

    return jax.shard_map(
        per_device, mesh=mesh, in_specs=in_specs, out_specs=out_specs, check_vma=False
    )
```

```python
import functools
import math

import jax
import jax.numpy as jnp
from jax import lax
from jax.experimental import pallas as pl
from jax.experimental.pallas import tpu as pltpu
from jax.sharding import PartitionSpec as P

NS_STEPS = 5
BF = jnp.bfloat16
F32 = jnp.float32
VMEM_BYTES = 60 * 1024 * 1024

def cost(us):
    return pl.CostEstimate(flops=1, bytes_accessed=int(us * 3.3e6) + 1, transcendentals=0)


COST_APPLY = cost(0)
COST_PACK = cost(0)
COST_GRADS = cost(0)
COST_ADD = cost(0)
COST_NEWTON = cost(0)
COST_PLACE = cost(0)

HBM = pl.BlockSpec(memory_space=pltpu.HBM)
ANY = pl.BlockSpec(memory_space=pl.ANY)
SMEM = pl.BlockSpec(memory_space=pltpu.SMEM)
VMEM = pl.BlockSpec(memory_space=pltpu.VMEM)

NZ = 4
PLANE = 8
DEVICES = NZ * PLANE


def newton_batch(xmat, width):
    for step in range(NS_STEPS):
        amat = jnp.einsum("mdf,mef->mde", xmat, xmat, preferred_element_type=F32).astype(BF)
        square = jnp.einsum("mde,mef->mdf", amat, amat, preferred_element_type=F32)
        bmat = (-4.775 * amat.astype(F32) + 2.0315 * square).astype(BF)
        nxt = 3.4445 * xmat.astype(F32) + jnp.einsum(
            "mde,mef->mdf", bmat, xmat, preferred_element_type=F32
        )
        if step == NS_STEPS - 1:
            nxt = nxt * (0.2 * math.sqrt(width))
        xmat = nxt.astype(BF)
    return xmat


def per_device_plain(queries, keys, values, token_rates, w_gate, w_up, w_down):
    head_count, head_size, hidden = w_gate.shape
    tokens = queries.shape[0]
    scale_one = head_size ** (-0.5)
    scale_two = hidden ** (-0.5)
    qpart = queries.reshape(tokens, head_count, head_size)
    kpart = keys.reshape(tokens, head_count, head_size)
    vpart = values.reshape(tokens, head_count, head_size)
    gq = scale_one * jnp.einsum("thd,hdf->htf", qpart, w_gate, preferred_element_type=F32)
    uq = scale_one * jnp.einsum("thd,hdf->htf", qpart, w_up, preferred_element_type=F32)
    hq = (jax.nn.silu(gq) * uq).astype(BF)
    applied = (
        scale_two * jnp.einsum("htf,hfd->thd", hq, w_down, preferred_element_type=F32)
    ).astype(BF)
    applied = applied.reshape(tokens, head_count * head_size)
    gk = scale_one * jnp.einsum("thd,hdf->htf", kpart, w_gate, preferred_element_type=F32)
    uk = scale_one * jnp.einsum("thd,hdf->htf", kpart, w_up, preferred_element_type=F32)
    hk = (jax.nn.silu(gk) * uk).astype(BF)
    vrate = (jnp.transpose(token_rates)[:, :, None] * vpart.astype(F32)).astype(BF)
    gdown = -scale_two * jnp.einsum("thd,htf->hdf", vrate, hk, preferred_element_type=F32)
    dhid = -scale_two * jnp.einsum("thd,hfd->htf", vrate, w_down, preferred_element_type=F32)
    sig = jax.nn.sigmoid(gk)
    dgate = (dhid * uk * sig * (1.0 + gk * (1.0 - sig))).astype(BF)
    dup = (dhid * jax.nn.silu(gk)).astype(BF)
    ggate = scale_one * jnp.einsum("thd,htf->hdf", kpart, dgate, preferred_element_type=F32)
    gup = scale_one * jnp.einsum("thd,htf->hdf", kpart, dup, preferred_element_type=F32)
    total = lax.psum(jnp.stack([ggate, gup, gdown], axis=1), "seq")
    norms = jnp.sqrt(jnp.sum(total * total, axis=(2, 3)))
    xmat = (total / (norms[:, :, None, None] + 1e-07)).astype(BF)
    result = newton_batch(xmat.reshape(head_count * 3, head_size, hidden), hidden)
    result = result.reshape(head_count, 3, head_size, hidden)
    return (applied, result[:, 0], result[:, 1], result[:, 2])


def sigmoid(x):
    return 0.5 * jnp.tanh(0.5 * x) + 0.5


def dot(a, b, dims=((1,), (0,))):
    return lax.dot_general(a, b, (dims, ((), ())), preferred_element_type=F32)


def applied_kernel(scale_one, scale_two, q_ref, wg_ref, wu_ref, wd_ref, out_ref):
    heads, size, _ = wg_ref.shape
    for head in range(heads):
        cols = slice(head * size, (head + 1) * size)
        q = q_ref[:, cols]
        gq = scale_one * dot(q, wg_ref[head])
        hq = (gq * sigmoid(gq) * dot(q, wu_ref[head])).astype(BF)
        out_ref[:, cols] = (scale_one * scale_two * dot(hq, wd_ref[head])).astype(BF)


def apply_queries(queries, w_gate, w_up, w_down):
    heads, size, hidden = w_gate.shape
    tokens = queries.shape[0]
    each = 4
    return pl.pallas_call(
        functools.partial(applied_kernel, size**-0.5, hidden**-0.5),
        grid=(heads // each,),
        out_shape=jax.ShapeDtypeStruct(queries.shape, BF),
        in_specs=[
            pl.BlockSpec((tokens, each * size), lambda h: (0, h)),
            pl.BlockSpec((each, size, hidden), lambda h: (h, 0, 0)),
            pl.BlockSpec((each, size, hidden), lambda h: (h, 0, 0)),
            pl.BlockSpec((each, hidden, size), lambda h: (h, 0, 0)),
        ],
        out_specs=pl.BlockSpec((tokens, each * size), lambda h: (0, h)),
        compiler_params=pltpu.CompilerParams(vmem_limit_bytes=VMEM_BYTES),
        cost_estimate=COST_APPLY,
        name="apply_queries",
    )(queries, w_gate, w_up, w_down)


def pack_kernel(size, k_ref, v_ref, rate_ref, *rest):
    out_ref = rest[-1]
    step = pl.program_id(0)
    lanes = lax.broadcasted_iota(jnp.int32, (rate_ref.shape[1], PLANE), 1)
    rates = jnp.transpose(rate_ref[...])
    for i in range(out_ref.shape[0]):
        cols = slice(i * size, (i + 1) * size)
        here = lanes == step * out_ref.shape[0] + i
        rate = jnp.sum(jnp.where(here, rates, 0.0), axis=1, keepdims=True)
        out_ref[i, 0] = k_ref[:, cols]
        out_ref[i, 1] = (rate * v_ref[:, cols].astype(F32)).astype(BF)


def pack_tokens(keys, values, rates, group, size, *follows):
    tokens = keys.shape[0]
    each = 4
    steps = PLANE // each
    return pl.pallas_call(
        functools.partial(pack_kernel, size),
        grid=(steps,),
        out_shape=jax.ShapeDtypeStruct((PLANE, 2, tokens, size), BF),
        in_specs=[
            pl.BlockSpec((tokens, each * size), lambda i: (0, group * steps + i)),
            pl.BlockSpec((tokens, each * size), lambda i: (0, group * steps + i)),
            pl.BlockSpec((PLANE, tokens), lambda i: (group, 0)),
        ]
        + [ANY] * len(follows),
        out_specs=pl.BlockSpec((each, 2, tokens, size), lambda i: (i, 0, 0, 0)),
        compiler_params=pltpu.CompilerParams(vmem_limit_bytes=16 * 1024 * 1024 if group else VMEM_BYTES),
        cost_estimate=COST_PACK,
        name="pack_tokens",
    )(keys, values, rates, *follows)


def grads_kernel(scale_one, scale_two, where_ref, wg_ref, wu_ref, wd_ref, blocks, *rest):
    keep, *send = rest[-7:-3]
    total, final, sem = rest[-3:]
    wg, wu = wg_ref[...], wu_ref[...]
    wdt = jnp.transpose(wd_ref[...])
    for b in range(0, PLANE, 2):
        k = blocks[b : b + 2, 0].reshape(2 * blocks.shape[2], blocks.shape[3])
        vr = blocks[b : b + 2, 1].reshape(2 * blocks.shape[2], blocks.shape[3])
        gk = scale_one * dot(k, wg)
        uk = dot(k, wu)
        dh = dot(vr, wdt)
        sig = sigmoid(gk)
        act = gk * sig
        hk = (act * uk).astype(BF)
        dg = (dh * uk * (sig + act * (1.0 - sig))).astype(BF)
        du = (dh * act).astype(BF)
        kt, vt = jnp.transpose(k), jnp.transpose(vr)
        parts = (dot(kt, dg), dot(kt, du), dot(vt, hk))
        for i in range(3):
            if b == 0:
                total[i] = parts[i]
            else:
                total[i] += parts[i]
    both = -scale_one * scale_two
    final[0] = (both * scale_one * total[0]).astype(BF)
    final[1] = (both * total[1]).astype(BF)
    final[2] = (both * total[2]).astype(BF)
    core, half = where_ref[4], final.shape[1] // 2
    mine = pl.ds(pl.multiple_of(core * half, half), half)
    others = pl.ds(pl.multiple_of((1 - core) * half, half), half)
    run_copies(
        [
            (final.at[1 - core, pl.ds(0, half)], send[0]),
            (final.at[1 - core, pl.ds(half, half)], send[1]),
            (final.at[2, others], send[2]),
            (final.at[core], keep.at[pl.ds(0, 2 * half)]),
            (final.at[2, mine], keep.at[pl.ds(2 * half, half)]),
        ],
        sem,
    )


def head_grads(where, blocks, weights, *follows):
    size, hidden = weights[0].shape
    return pl.pallas_call(
        functools.partial(grads_kernel, size**-0.5, hidden**-0.5),
        out_shape=[jax.ShapeDtypeStruct((size + size // 2, hidden), BF)]
        + [jax.ShapeDtypeStruct((size // 2, hidden), BF)] * 3,
        in_specs=[SMEM] + [VMEM] * 4 + [ANY] * len(follows),
        out_specs=[ANY] * 4,
        scratch_shapes=[
            pltpu.VMEM((3, size, hidden), F32),
            pltpu.VMEM((3, size, hidden), BF),
            pltpu.SemaphoreType.DMA((5,)),
        ],
        compiler_params=pltpu.CompilerParams(vmem_limit_bytes=24 * 1024 * 1024),
        cost_estimate=COST_GRADS,
        name="head_grads",
    )(where, *weights, blocks, *follows)


def combine_kernel(keep_ref, a_ref, b_ref, c_ref, *rest):
    out_ref, part_ref = rest[-2:]
    rows = part_ref.shape[0]
    for i, ref in enumerate((a_ref, b_ref, c_ref)):
        at = slice(i * rows, (i + 1) * rows)
        total = (keep_ref[at].astype(F32) + ref[...].astype(F32)).astype(BF)
        out_ref[at] = total
    part_ref[...] = total


def combine(keep, parts, *follows):
    return pl.pallas_call(
        combine_kernel,
        out_shape=[
            jax.ShapeDtypeStruct(keep.shape, BF),
            jax.ShapeDtypeStruct(parts[-1].shape, BF),
        ],
        in_specs=[VMEM] * 4 + [ANY] * len(follows),
        out_specs=[VMEM] * 2,
        compiler_params=pltpu.CompilerParams(vmem_limit_bytes=8 * 1024 * 1024),
        cost_estimate=COST_ADD,
        name="add_partials",
    )(keep, *parts, *follows)


def newton_kernel(where_ref, *rest):
    mine_ref, other_ref, mine_sib, other_sib = rest[:4]
    out_ref, total, held = rest[-3:]
    size, width = held.shape
    half = size // 2
    core = where_ref[4]
    mine = pl.ds(pl.multiple_of(core * half, half), half)
    others = pl.ds(pl.multiple_of((1 - core) * half, half), half)
    total[mine, :] = mine_ref[size:].astype(F32) + other_ref[size:].astype(F32)
    total[others, :] = mine_sib[...].astype(F32) + other_sib[...].astype(F32)
    mats = []
    main = mine_ref[:size].astype(F32) + other_ref[:size].astype(F32)
    for grad in (main, total[...]):
        norm = jnp.sqrt(jnp.sum(grad * grad))
        mats.append((grad / (norm + 1e-07)).astype(BF))
    for step in range(NS_STEPS):
        squares = [dot(x, x, ((1,), (1,))).astype(BF) for x in mats]
        mixes = [
            (-4.775 * a.astype(F32) + 2.0315 * dot(a, a)).astype(BF) for a in squares
        ]
        nexts = [3.4445 * x.astype(F32) + dot(b, x) for b, x in zip(mixes, mats)]
        if step == NS_STEPS - 1:
            nexts = [n * (0.2 * math.sqrt(width)) for n in nexts]
        mats = [n.astype(BF) for n in nexts]
    out_ref[:size] = mats[0]
    held[...] = mats[1]
    out_ref[size:] = held[mine, :]


def newton(where, parts, *follows):
    rows, hidden = parts[0].shape
    size = rows * 2 // 3
    return pl.pallas_call(
        newton_kernel,
        out_shape=jax.ShapeDtypeStruct((rows, hidden), BF),
        in_specs=[SMEM] + [VMEM] * len(parts) + [ANY] * len(follows),
        out_specs=VMEM,
        scratch_shapes=[pltpu.VMEM((size, hidden), F32), pltpu.VMEM((size, hidden), BF)],
        compiler_params=pltpu.CompilerParams(vmem_limit_bytes=20 * 1024 * 1024),
        cost_estimate=COST_NEWTON,
        name="newton_schulz",
    )(where, *parts, *follows)


def run_copies(pairs, sem):
    copies = [pltpu.make_async_copy(a, b, sem.at[i]) for i, (a, b) in enumerate(pairs)]
    for copy in copies:
        copy.start()
    for copy in copies:
        copy.wait()


def place_kernel(group, which, size, where_ref, *rest):
    blocks, (gate, up, down, sem) = rest[: len(which)], rest[-4:]
    z, y, x, core = (where_ref[i] for i in range(1, 5))
    half = size // 2

    def put(parity):
        pairs = []
        for i, block in zip(which, blocks):
            flip, other, kind = i // 8, i // 4 % 2, i % 4
            side, c = (1 - parity, 1 - core) if other else (parity, core)
            at = ((y, x), (y ^ (1 - c), x ^ c), (y ^ c, x ^ (1 - c)), (1 - y, 1 - x))[kind]
            head = group * PLANE + (lax.rem(z, 2) ^ flip) * 4 + at[0] * 2 + at[1]
            m0 = up if side else gate
            pairs.append((block.at[pl.ds(0, size)], m0.at[head]))
            pairs.append((block.at[pl.ds(size, half)], down.at[head, pl.ds(side * half, half)]))
        run_copies(pairs, sem)

    for parity in range(2):

        @pl.when(core == parity)
        def _():
            put(parity)


def place(where, blocks, steps, shape, group, which=tuple(range(16))):
    count = len(blocks)
    return pl.pallas_call(
        functools.partial(place_kernel, group, which, shape[1]),
        out_shape=[jax.ShapeDtypeStruct(shape, BF)] * 3,
        in_specs=[SMEM] + [VMEM] * count + [ANY] * len(steps),
        out_specs=[ANY] * 3,
        scratch_shapes=[pltpu.SemaphoreType.DMA((2 * count,))],
        input_output_aliases={1 + count + i: i for i in range(len(steps))},
        compiler_params=pltpu.CompilerParams(vmem_limit_bytes=16 * 1024 * 1024),
        cost_estimate=COST_PLACE,
        name="place_steps",
    )(where, *blocks, *steps)


def permutation(target):
    pairs = []
    for i in range(DEVICES):
        z, y, x, core = target(i // 8, i // 4 % 2, i // 2 % 2, i % 2)
        pairs.append((i, ((z * 2 + y) * 2 + x) * 2 + core))
    return pairs


CUBES = [
    [((2 * zhi + zlo) * 4 + yx) * 2 + core for zlo in range(2) for yx in range(4)]
    for zhi in range(2)
    for core in range(2)
]
Z_MOVES = [permutation(lambda z, y, x, c, s=s: (z ^ s, y, x, c)) for s in range(NZ)]
FIRST_MOVE = permutation(lambda z, y, x, c: (z, y ^ (1 - c), x ^ c, c))
SECOND_MOVE = permutation(lambda z, y, x, c: (z, y ^ c, x ^ (1 - c), c))
CORE_MOVE = permutation(lambda z, y, x, c: (z, y, x, 1 - c))


def move(array, pairs):
    return lax.ppermute(array, "seq", pairs)


def after(array, *others):
    return lax.optimization_barrier((array, *others))[0]


def per_device_fast(queries, keys, values, token_rates, w_gate, w_up, w_down):
    heads, size, hidden = w_gate.shape
    groups = heads // PLANE
    index = lax.axis_index("seq")
    z, core = index // 8, index % 2
    y, x = index // 4 % 2, index // 2 % 2
    where = jnp.stack([z % 2 * 4 + y * 2 + x, z, y, x, core]).astype(jnp.int32)

    packed = [pack_tokens(keys, values, token_rates, 0, size)]
    applied = apply_queries(queries, w_gate, w_up, w_down)
    weights = [
        [lax.dynamic_index_in_dim(w, g * PLANE + where[0], 0, False) for w in (w_gate, w_up, w_down)]
        for g in range(groups)
    ]
    packed.append(pack_tokens(keys, values, token_rates, 1, size, applied, *weights[0], *weights[1]))
    received = [
        lax.all_to_all(block, "seq", 0, 0, axis_index_groups=CUBES, tiled=True)
        for block in packed
    ]

    def summed(group, waits, *follow):
        keep, *send = head_grads(where, received[group], weights[group], *follow)
        return combine(keep, [move(block, CORE_MOVE) for block in send], *waits)

    def round_two(one, two, far):
        return move(one, Z_MOVES[1]), move(two, FIRST_MOVE), move(far, SECOND_MOVE)

    def with_sibling(*gathered):
        return [*gathered] + [move(block, CORE_MOVE) for block in gathered]

    mine, part = summed(0, ())
    other = move(mine, Z_MOVES[2])
    parts = (mine, other, move(part, CORE_MOVE), move(other[size:], CORE_MOVE))
    mine_b, part_b = summed(1, (other,), mine)
    other_b = move(mine_b, Z_MOVES[2])
    near = newton(where, parts, mine_b)
    one, two, far = (move(near, to) for to in (FIRST_MOVE, SECOND_MOVE, Z_MOVES[1]))
    one, two, other_b = lax.optimization_barrier((one, two, other_b))
    far_one, three = move(one, Z_MOVES[1]), move(two, FIRST_MOVE)
    parts = (mine_b, other_b, move(part_b, CORE_MOVE), move(other_b[size:], CORE_MOVE))
    near_b = newton(where, parts)
    near_b, three, far = lax.optimization_barrier((near_b, three, far))
    far_two = move(far, SECOND_MOVE)
    far_three = move(far_one, SECOND_MOVE)
    one_b, two_b, far_b = (move(near_b, to) for to in (FIRST_MOVE, SECOND_MOVE, Z_MOVES[1]))
    blocks = with_sibling(near, one, two, three)
    one, two, far_b, far_two, far_three = lax.optimization_barrier(
        (one_b, two_b, far_b, far_two, far_three)
    )
    blocks += with_sibling(far, far_one, far_two, far_three)
    steps = place(where, blocks, (), w_gate.shape, 0)
    far_one, three, far_two = round_two(one, two, far_b)
    far_one, three, far_two = lax.optimization_barrier((far_one, three, far_two))
    far_three = move(far_one, SECOND_MOVE)
    blocks = with_sibling(near_b, one, two, three) + with_sibling(far_b, far_one, far_two)
    which = (*range(11), 12, 13, 14)
    steps = place(where, blocks, steps, w_gate.shape, 1, which)
    far_three, *steps = lax.optimization_barrier((far_three, *steps))
    steps = place(where, with_sibling(far_three), steps, w_gate.shape, 1, (11, 15))
    return (applied, *steps)


def solution(mesh):
    in_specs = (
        P("seq", "head"),
        P("seq", "head"),
        P("seq", "head"),
        P("head", "seq"),
        P("head", None, None),
        P("head", None, None),
        P("head", None, None),
    )
    out_specs = (
        P("seq", "head"),
        P("head", None, None),
        P("head", None, None),
        P("head", None, None),
    )
    sizes = mesh.shape

    def per_device(*args):
        heads = args[4].shape[0]
        fast = sizes["seq"] == DEVICES and heads == 2 * PLANE
        return (per_device_fast if fast else per_device_plain)(*args)

    return jax.shard_map(
        per_device, mesh=mesh, in_specs=in_specs, out_specs=out_specs, check_vma=False
    )
```

```python
import functools
import math

import jax
import jax.numpy as jnp
from jax import lax
from jax.experimental import pallas as pl
from jax.experimental.pallas import tpu as pltpu
from jax.sharding import PartitionSpec as P

NS_STEPS = 5
BF = jnp.bfloat16
F32 = jnp.float32
VMEM_BYTES = 60 * 1024 * 1024

def cost(us):
    return pl.CostEstimate(flops=1, bytes_accessed=int(us * 3.3e6) + 1, transcendentals=0)


COST_APPLY = cost(0)
COST_PACK = cost(0)
COST_GRADS = cost(0)
COST_ADD = cost(0)
COST_NEWTON = cost(0)
COST_PLACE = cost(0)

HBM = pl.BlockSpec(memory_space=pltpu.HBM)
ANY = pl.BlockSpec(memory_space=pl.ANY)
SMEM = pl.BlockSpec(memory_space=pltpu.SMEM)
VMEM = pl.BlockSpec(memory_space=pltpu.VMEM)

NZ = 4
PLANE = 8
DEVICES = NZ * PLANE


def newton_batch(xmat, width):
    for step in range(NS_STEPS):
        amat = jnp.einsum("mdf,mef->mde", xmat, xmat, preferred_element_type=F32).astype(BF)
        square = jnp.einsum("mde,mef->mdf", amat, amat, preferred_element_type=F32)
        bmat = (-4.775 * amat.astype(F32) + 2.0315 * square).astype(BF)
        nxt = 3.4445 * xmat.astype(F32) + jnp.einsum(
            "mde,mef->mdf", bmat, xmat, preferred_element_type=F32
        )
        if step == NS_STEPS - 1:
            nxt = nxt * (0.2 * math.sqrt(width))
        xmat = nxt.astype(BF)
    return xmat


def per_device_plain(queries, keys, values, token_rates, w_gate, w_up, w_down):
    head_count, head_size, hidden = w_gate.shape
    tokens = queries.shape[0]
    scale_one = head_size ** (-0.5)
    scale_two = hidden ** (-0.5)
    qpart = queries.reshape(tokens, head_count, head_size)
    kpart = keys.reshape(tokens, head_count, head_size)
    vpart = values.reshape(tokens, head_count, head_size)
    gq = scale_one * jnp.einsum("thd,hdf->htf", qpart, w_gate, preferred_element_type=F32)
    uq = scale_one * jnp.einsum("thd,hdf->htf", qpart, w_up, preferred_element_type=F32)
    hq = (jax.nn.silu(gq) * uq).astype(BF)
    applied = (
        scale_two * jnp.einsum("htf,hfd->thd", hq, w_down, preferred_element_type=F32)
    ).astype(BF)
    applied = applied.reshape(tokens, head_count * head_size)
    gk = scale_one * jnp.einsum("thd,hdf->htf", kpart, w_gate, preferred_element_type=F32)
    uk = scale_one * jnp.einsum("thd,hdf->htf", kpart, w_up, preferred_element_type=F32)
    hk = (jax.nn.silu(gk) * uk).astype(BF)
    vrate = (jnp.transpose(token_rates)[:, :, None] * vpart.astype(F32)).astype(BF)
    gdown = -scale_two * jnp.einsum("thd,htf->hdf", vrate, hk, preferred_element_type=F32)
    dhid = -scale_two * jnp.einsum("thd,hfd->htf", vrate, w_down, preferred_element_type=F32)
    sig = jax.nn.sigmoid(gk)
    dgate = (dhid * uk * sig * (1.0 + gk * (1.0 - sig))).astype(BF)
    dup = (dhid * jax.nn.silu(gk)).astype(BF)
    ggate = scale_one * jnp.einsum("thd,htf->hdf", kpart, dgate, preferred_element_type=F32)
    gup = scale_one * jnp.einsum("thd,htf->hdf", kpart, dup, preferred_element_type=F32)
    total = lax.psum(jnp.stack([ggate, gup, gdown], axis=1), "seq")
    norms = jnp.sqrt(jnp.sum(total * total, axis=(2, 3)))
    xmat = (total / (norms[:, :, None, None] + 1e-07)).astype(BF)
    result = newton_batch(xmat.reshape(head_count * 3, head_size, hidden), hidden)
    result = result.reshape(head_count, 3, head_size, hidden)
    return (applied, result[:, 0], result[:, 1], result[:, 2])


def sigmoid(x):
    return 0.5 * jnp.tanh(0.5 * x) + 0.5


def dot(a, b, dims=((1,), (0,))):
    return lax.dot_general(a, b, (dims, ((), ())), preferred_element_type=F32)


def applied_kernel(scale_one, scale_two, q_ref, wg_ref, wu_ref, wd_ref, out_ref):
    heads, size, _ = wg_ref.shape
    for head in range(heads):
        cols = slice(head * size, (head + 1) * size)
        q = q_ref[:, cols]
        gq = scale_one * dot(q, wg_ref[head])
        hq = (gq * sigmoid(gq) * dot(q, wu_ref[head])).astype(BF)
        out_ref[:, cols] = (scale_one * scale_two * dot(hq, wd_ref[head])).astype(BF)


def apply_queries(queries, w_gate, w_up, w_down):
    heads, size, hidden = w_gate.shape
    tokens = queries.shape[0]
    each = 4
    return pl.pallas_call(
        functools.partial(applied_kernel, size**-0.5, hidden**-0.5),
        grid=(heads // each,),
        out_shape=jax.ShapeDtypeStruct(queries.shape, BF),
        in_specs=[
            pl.BlockSpec((tokens, each * size), lambda h: (0, h)),
            pl.BlockSpec((each, size, hidden), lambda h: (h, 0, 0)),
            pl.BlockSpec((each, size, hidden), lambda h: (h, 0, 0)),
            pl.BlockSpec((each, hidden, size), lambda h: (h, 0, 0)),
        ],
        out_specs=pl.BlockSpec((tokens, each * size), lambda h: (0, h)),
        compiler_params=pltpu.CompilerParams(vmem_limit_bytes=VMEM_BYTES),
        cost_estimate=COST_APPLY,
        name="apply_queries",
    )(queries, w_gate, w_up, w_down)


def pack_kernel(size, k_ref, v_ref, rate_ref, *rest):
    out_ref = rest[-1]
    step = pl.program_id(0)
    lanes = lax.broadcasted_iota(jnp.int32, (rate_ref.shape[1], PLANE), 1)
    rates = jnp.transpose(rate_ref[...])
    for i in range(out_ref.shape[0]):
        cols = slice(i * size, (i + 1) * size)
        here = lanes == step * out_ref.shape[0] + i
        rate = jnp.sum(jnp.where(here, rates, 0.0), axis=1, keepdims=True)
        out_ref[i, 0] = k_ref[:, cols]
        out_ref[i, 1] = (rate * v_ref[:, cols].astype(F32)).astype(BF)


def pack_tokens(keys, values, rates, group, size, *follows):
    tokens = keys.shape[0]
    each = 4
    steps = PLANE // each
    return pl.pallas_call(
        functools.partial(pack_kernel, size),
        grid=(steps,),
        out_shape=jax.ShapeDtypeStruct((PLANE, 2, tokens, size), BF),
        in_specs=[
            pl.BlockSpec((tokens, each * size), lambda i: (0, group * steps + i)),
            pl.BlockSpec((tokens, each * size), lambda i: (0, group * steps + i)),
            pl.BlockSpec((PLANE, tokens), lambda i: (group, 0)),
        ]
        + [ANY] * len(follows),
        out_specs=pl.BlockSpec((each, 2, tokens, size), lambda i: (i, 0, 0, 0)),
        compiler_params=pltpu.CompilerParams(vmem_limit_bytes=16 * 1024 * 1024 if group else VMEM_BYTES),
        cost_estimate=COST_PACK,
        name="pack_tokens",
    )(keys, values, rates, *follows)


def grads_kernel(scale_one, scale_two, where_ref, w_ref, blocks, *rest):
    keep, *send = rest[-7:-3]
    total, final, sem = rest[-3:]
    wg, wu, wdt = w_ref[0], w_ref[1], w_ref[2]
    for b in range(0, PLANE, 2):
        k = blocks[b : b + 2, 0].reshape(2 * blocks.shape[2], blocks.shape[3])
        vr = blocks[b : b + 2, 1].reshape(2 * blocks.shape[2], blocks.shape[3])
        gk = scale_one * dot(k, wg)
        uk = dot(k, wu)
        dh = dot(vr, wdt)
        sig = sigmoid(gk)
        act = gk * sig
        hk = (act * uk).astype(BF)
        dg = (dh * uk * (sig + act * (1.0 - sig))).astype(BF)
        du = (dh * act).astype(BF)
        kt, vt = jnp.transpose(k), jnp.transpose(vr)
        parts = (dot(kt, dg), dot(kt, du), dot(vt, hk))
        for i in range(3):
            if b == 0:
                total[i] = parts[i]
            else:
                total[i] += parts[i]
    both = -scale_one * scale_two
    final[0] = (both * scale_one * total[0]).astype(BF)
    final[1] = (both * total[1]).astype(BF)
    final[2] = (both * total[2]).astype(BF)
    core, half = where_ref[4], final.shape[1] // 2
    mine = pl.ds(pl.multiple_of(core * half, half), half)
    others = pl.ds(pl.multiple_of((1 - core) * half, half), half)
    run_copies(
        [
            (final.at[1 - core, pl.ds(0, half)], send[0]),
            (final.at[1 - core, pl.ds(half, half)], send[1]),
            (final.at[2, others], send[2]),
            (final.at[core], keep.at[pl.ds(0, 2 * half)]),
            (final.at[2, mine], keep.at[pl.ds(2 * half, half)]),
        ],
        sem,
    )


def head_grads(where, blocks, weights, *follows):
    _, size, hidden = weights[0].shape
    return pl.pallas_call(
        functools.partial(grads_kernel, size**-0.5, hidden**-0.5),
        out_shape=[jax.ShapeDtypeStruct((size + size // 2, hidden), BF)]
        + [jax.ShapeDtypeStruct((size // 2, hidden), BF)] * 3,
        in_specs=[SMEM] + [VMEM] * 2 + [ANY] * len(follows),
        out_specs=[ANY] * 4,
        scratch_shapes=[
            pltpu.VMEM((3, size, hidden), F32),
            pltpu.VMEM((3, size, hidden), BF),
            pltpu.SemaphoreType.DMA((5,)),
        ],
        compiler_params=pltpu.CompilerParams(vmem_limit_bytes=24 * 1024 * 1024),
        cost_estimate=COST_GRADS,
        name="head_grads",
    )(where, *weights, blocks, *follows)


def combine_kernel(keep_ref, a_ref, b_ref, c_ref, *rest):
    out_ref, part_ref = rest[-2:]
    rows = part_ref.shape[0]
    for i, ref in enumerate((a_ref, b_ref, c_ref)):
        at = slice(i * rows, (i + 1) * rows)
        total = (keep_ref[at].astype(F32) + ref[...].astype(F32)).astype(BF)
        out_ref[at] = total
    part_ref[...] = total


def combine(keep, parts, *follows):
    return pl.pallas_call(
        combine_kernel,
        out_shape=[
            jax.ShapeDtypeStruct(keep.shape, BF),
            jax.ShapeDtypeStruct(parts[-1].shape, BF),
        ],
        in_specs=[VMEM] * 4 + [ANY] * len(follows),
        out_specs=[VMEM] * 2,
        compiler_params=pltpu.CompilerParams(vmem_limit_bytes=8 * 1024 * 1024),
        cost_estimate=COST_ADD,
        name="add_partials",
    )(keep, *parts, *follows)


def newton_kernel(where_ref, *rest):
    mine_ref, other_ref, mine_sib, other_sib = rest[:4]
    out_ref, total, held = rest[-3:]
    size, width = held.shape
    half = size // 2
    core = where_ref[4]
    mine = pl.ds(pl.multiple_of(core * half, half), half)
    others = pl.ds(pl.multiple_of((1 - core) * half, half), half)
    total[mine, :] = mine_ref[size:].astype(F32) + other_ref[size:].astype(F32)
    total[others, :] = mine_sib[...].astype(F32) + other_sib[...].astype(F32)
    mats = []
    main = mine_ref[:size].astype(F32) + other_ref[:size].astype(F32)
    for grad in (main, total[...]):
        norm = jnp.sqrt(jnp.sum(grad * grad))
        mats.append((grad / (norm + 1e-07)).astype(BF))
    for step in range(NS_STEPS):
        squares = [dot(x, x, ((1,), (1,))).astype(BF) for x in mats]
        mixes = [
            (-4.775 * a.astype(F32) + 2.0315 * dot(a, a)).astype(BF) for a in squares
        ]
        nexts = [3.4445 * x.astype(F32) + dot(b, x) for b, x in zip(mixes, mats)]
        if step == NS_STEPS - 1:
            nexts = [n * (0.2 * math.sqrt(width)) for n in nexts]
        mats = [n.astype(BF) for n in nexts]
    out_ref[:size] = mats[0]
    held[...] = mats[1]
    out_ref[size:] = held[mine, :]


def newton(where, parts, *follows):
    rows, hidden = parts[0].shape
    size = rows * 2 // 3
    return pl.pallas_call(
        newton_kernel,
        out_shape=jax.ShapeDtypeStruct((rows, hidden), BF),
        in_specs=[SMEM] + [VMEM] * len(parts) + [ANY] * len(follows),
        out_specs=VMEM,
        scratch_shapes=[pltpu.VMEM((size, hidden), F32), pltpu.VMEM((size, hidden), BF)],
        compiler_params=pltpu.CompilerParams(vmem_limit_bytes=20 * 1024 * 1024),
        cost_estimate=COST_NEWTON,
        name="newton_schulz",
    )(where, *parts, *follows)


def run_copies(pairs, sem):
    copies = [pltpu.make_async_copy(a, b, sem.at[i]) for i, (a, b) in enumerate(pairs)]
    for copy in copies:
        copy.start()
    for copy in copies:
        copy.wait()


def place_kernel(group, which, size, where_ref, *rest):
    blocks, (gate, up, down, sem) = rest[: len(which)], rest[-4:]
    z, y, x, core = (where_ref[i] for i in range(1, 5))
    half = size // 2

    def put(parity):
        pairs = []
        for i, block in zip(which, blocks):
            flip, other, kind = i // 8, i // 4 % 2, i % 4
            side, c = (1 - parity, 1 - core) if other else (parity, core)
            at = ((y, x), (y ^ (1 - c), x ^ c), (y ^ c, x ^ (1 - c)), (1 - y, 1 - x))[kind]
            head = group * PLANE + (lax.rem(z, 2) ^ flip) * 4 + at[0] * 2 + at[1]
            m0 = up if side else gate
            pairs.append((block.at[pl.ds(0, size)], m0.at[head]))
            pairs.append((block.at[pl.ds(size, half)], down.at[head, pl.ds(side * half, half)]))
        run_copies(pairs, sem)

    for parity in range(2):

        @pl.when(core == parity)
        def _():
            put(parity)


def place(where, blocks, steps, shape, group, which=tuple(range(16))):
    count = len(blocks)
    return pl.pallas_call(
        functools.partial(place_kernel, group, which, shape[1]),
        out_shape=[jax.ShapeDtypeStruct(shape, BF)] * 3,
        in_specs=[SMEM] + [VMEM] * count + [ANY] * len(steps),
        out_specs=[ANY] * 3,
        scratch_shapes=[pltpu.SemaphoreType.DMA((2 * count,))],
        input_output_aliases={1 + count + i: i for i in range(len(steps))},
        compiler_params=pltpu.CompilerParams(vmem_limit_bytes=16 * 1024 * 1024),
        cost_estimate=COST_PLACE,
        name="place_steps",
    )(where, *blocks, *steps)


def permutation(target):
    pairs = []
    for i in range(DEVICES):
        z, y, x, core = target(i // 8, i // 4 % 2, i // 2 % 2, i % 2)
        pairs.append((i, ((z * 2 + y) * 2 + x) * 2 + core))
    return pairs


CUBES = [
    [((2 * zhi + zlo) * 4 + yx) * 2 + core for zlo in range(2) for yx in range(4)]
    for zhi in range(2)
    for core in range(2)
]
Z_MOVES = [permutation(lambda z, y, x, c, s=s: (z ^ s, y, x, c)) for s in range(NZ)]
FIRST_MOVE = permutation(lambda z, y, x, c: (z, y ^ (1 - c), x ^ c, c))
SECOND_MOVE = permutation(lambda z, y, x, c: (z, y ^ c, x ^ (1 - c), c))
CORE_MOVE = permutation(lambda z, y, x, c: (z, y, x, 1 - c))


def move(array, pairs):
    return lax.ppermute(array, "seq", pairs)


def after(array, *others):
    return lax.optimization_barrier((array, *others))[0]


def per_device_fast(queries, keys, values, token_rates, w_gate, w_up, w_down):
    heads, size, hidden = w_gate.shape
    groups = heads // PLANE
    index = lax.axis_index("seq")
    z, core = index // 8, index % 2
    y, x = index // 4 % 2, index // 2 % 2
    where = jnp.stack([z % 2 * 4 + y * 2 + x, z, y, x, core]).astype(jnp.int32)

    packed = [pack_tokens(keys, values, token_rates, 0, size)]
    applied = apply_queries(queries, w_gate, w_up, w_down)
    weights = []
    for group in range(groups):
        gate, up, down = (
            lax.dynamic_index_in_dim(w, group * PLANE + where[0], 0, False)
            for w in (w_gate, w_up, w_down)
        )
        weights.append((jnp.stack([gate, up, jnp.transpose(down)]),))
    packed.append(pack_tokens(keys, values, token_rates, 1, size, applied, *weights[0], *weights[1]))
    received = [
        lax.all_to_all(block, "seq", 0, 0, axis_index_groups=CUBES, tiled=True)
        for block in packed
    ]

    def summed(group, waits, *follow):
        keep, *send = head_grads(where, received[group], weights[group], *follow)
        return combine(keep, [move(block, CORE_MOVE) for block in send], *waits)

    def round_two(one, two, far):
        return move(one, Z_MOVES[1]), move(two, FIRST_MOVE), move(far, SECOND_MOVE)

    def with_sibling(*gathered):
        return [*gathered] + [move(block, CORE_MOVE) for block in gathered]

    mine, part = summed(0, ())
    other = move(mine, Z_MOVES[2])
    parts = (mine, other, move(part, CORE_MOVE), move(other[size:], CORE_MOVE))
    mine_b, part_b = summed(1, (other,), mine)
    other_b = move(mine_b, Z_MOVES[2])
    near = newton(where, parts, mine_b)
    one, two, far = (move(near, to) for to in (FIRST_MOVE, SECOND_MOVE, Z_MOVES[1]))
    one, two, other_b = lax.optimization_barrier((one, two, other_b))
    far_one, three = move(one, Z_MOVES[1]), move(two, FIRST_MOVE)
    parts = (mine_b, other_b, move(part_b, CORE_MOVE), move(other_b[size:], CORE_MOVE))
    near_b = newton(where, parts)
    near_b, three, far = lax.optimization_barrier((near_b, three, far))
    far_two = move(far, SECOND_MOVE)
    far_three = move(far_one, SECOND_MOVE)
    one_b, two_b, far_b = (move(near_b, to) for to in (FIRST_MOVE, SECOND_MOVE, Z_MOVES[1]))
    blocks = with_sibling(near, one, two, three)
    one, two, far_b, far_two, far_three = lax.optimization_barrier(
        (one_b, two_b, far_b, far_two, far_three)
    )
    blocks += with_sibling(far, far_one, far_two, far_three)
    steps = place(where, blocks, (), w_gate.shape, 0)
    far_one, three, far_two = round_two(one, two, far_b)
    far_one, three, far_two = lax.optimization_barrier((far_one, three, far_two))
    far_three = move(far_one, SECOND_MOVE)
    blocks = with_sibling(near_b, one, two, three) + with_sibling(far_b, far_one, far_two)
    which = (*range(11), 12, 13, 14)
    steps = place(where, blocks, steps, w_gate.shape, 1, which)
    far_three, *steps = lax.optimization_barrier((far_three, *steps))
    steps = place(where, with_sibling(far_three), steps, w_gate.shape, 1, (11, 15))
    return (applied, *steps)


def solution(mesh):
    in_specs = (
        P("seq", "head"),
        P("seq", "head"),
        P("seq", "head"),
        P("head", "seq"),
        P("head", None, None),
        P("head", None, None),
        P("head", None, None),
    )
    out_specs = (
        P("seq", "head"),
        P("head", None, None),
        P("head", None, None),
        P("head", None, None),
    )
    sizes = mesh.shape

    def per_device(*args):
        heads = args[4].shape[0]
        fast = sizes["seq"] == DEVICES and heads == 2 * PLANE
        return (per_device_fast if fast else per_device_plain)(*args)

    return jax.shard_map(
        per_device, mesh=mesh, in_specs=in_specs, out_specs=out_specs, check_vma=False
    )
```
